256 devices in a mesh: rep: 16 (over z, core), tp: 16 (over x, y).
Axes of the slice: x: 4, y: 4, z: 8, core: 2. Of those that a mesh axis runs over, the one named last changes fastest.
Arguments:
- tokens: bfloat16 [16, 3072, 4096], P('rep', 'tp'), may hold values from -6 to 6
- out_grad: bfloat16 [16, 3072, 2048], P('rep', None, 'tp'), may hold values from -0.109375 to 0.109375
- weights: float32 [2048, 4096], P('tp'), may hold values from -6 to 6
- moment_one: bfloat16 [16, 2048, 4096], P('rep', 'tp'), may hold values from -3 to 3
- moment_two: bfloat16 [16, 2048, 4096], P('rep', 'tp'), may hold values from 0.0019989014 to 0.019897461
- error_buf: bfloat16 [16, 2048, 4096], P('rep', 'tp'), may hold values from -6 to 6
- momentum: bfloat16 [2048, 4096], P('tp'), may hold values from -6 to 6
- tile_lists: int32 [16, 16, 4], P('rep', 'tp'), may hold values from -1 to 31, as said below
Outputs:
- weights_new: float32 [2048, 4096], P('tp')
- error_new: bfloat16 [16, 2048, 4096], P('rep', 'tp')
- momentum_new: bfloat16 [2048, 4096], P('tp')
The draws below stay inside these ranges and needn't reach their ends.
Inputs may be any that keep to these rules, and one draw needn't show every extreme that they name: Each list tile_lists[r, j] holds between 0 and 4 distinct tile numbers below 32 in its first slots and -1 in the rest; in every replica some list holds exactly 4; the number of listed tiles may differ from list to list.
All inputs are finite; a program needn't handle non-finite values.
Results may differ from the reference program's by a relative error of at most 0.0065.
Values may be sent and summed in bfloat16 or wider, within the bound.
No kernel may reach another device: no remote copies, remote signals or barrier semaphores. Data moves between devices by JAX's collectives and lax.ppermute only.
A program may use at most 128 MiB of HBM per device.

```python
import math
import jax
import jax.numpy as jnp

D = 4096
COLS_DEV = 128
TILE = 128
K_MAX = 4
REPS = 16
COLS = 2048
TOKENS = 3072
TILES_DEV = 32
N_TP = 16


def draw_tile_lists(key, part):
    key = jax.random.fold_in(key, 7)
    key_order = jax.random.fold_in(key, 1)
    key_count = jax.random.fold_in(key, 2)
    scores = jax.random.randint(key_order, (REPS, N_TP, TILES_DEV), 0, 1 << 20) * TILES_DEV + jnp.arange(TILES_DEV, dtype=jnp.int32)
    order = jnp.argsort(scores, axis=-1).astype(jnp.int32)[:, :, :K_MAX]
    table = jnp.minimum(jnp.array([2, 3, 3, 4, 4, 4, 4, 4], dtype=jnp.int32), K_MAX)
    counts = table[jax.random.randint(key_count, (REPS, N_TP), 0, 8)]
    filled = jnp.arange(N_TP, dtype=jnp.int32)[None, :] == (jnp.arange(REPS, dtype=jnp.int32) % N_TP)[:, None]
    counts = jnp.where(filled, K_MAX, counts)
    slots = jnp.arange(K_MAX, dtype=jnp.int32)
    return jnp.where(slots[None, None, :] < counts[:, :, None], order, -1).astype(jnp.int32)


def shard_levels(own_key, shape, cuts, least, largest):
    level, own = 1.0, jax.random.fold_in(own_key, 6)
    for dim, blocks in cuts:
        heights = jnp.exp(jax.random.uniform(jax.random.fold_in(own, dim), (blocks,), jnp.float32, least / len(cuts), largest / len(cuts)))
        level = level * jnp.repeat(heights, shape[dim] // blocks).reshape([-1 if axis == dim else 1 for axis in range(len(shape))])
    return level


def normal_values(key, shape, spread, reach, shards=(), held_as=jnp.bfloat16):
    level = shard_levels(key, shape, shards, -0.22, 0.18) if shards else 1.0
    drawn = jax.random.normal(key, shape, jnp.float32) * spread * level
    return jnp.minimum(jnp.maximum(drawn, -reach), reach).astype(held_as)


def setup_inputs(seed: int = 0) -> dict:
    splits = jax.random.split(jax.random.key(seed), 9)
    return {
        "tokens": normal_values(splits[0], (REPS, TOKENS, D), 1.0, 6.0, ((0, 16), (1, 16))),
        "out_grad": normal_values(splits[1], (REPS, TOKENS, COLS), TOKENS ** -0.5, 0.109375, ((0, 16), (2, 16))),
        "weights": normal_values(splits[2], (COLS, D), 1.0, 6.0, ((0, 16),), jnp.float32),
        "moment_one": normal_values(splits[3], (REPS, COLS, D), 0.2, 3.0, ((0, 16), (1, 16))),
        "moment_two": jnp.clip(jnp.exp(math.log(0.019897461) - 2.2979944 * jax.random.uniform(splits[4], (REPS, COLS, D), jnp.float32) ** shard_levels(splits[4], (REPS, COLS, D), ((0, 16), (1, 16)), -0.2, 0.2)), 0.0019989014, 0.019897461).astype(jnp.bfloat16),
        "error_buf": normal_values(splits[5], (REPS, COLS, D), 1.0, 6.0, ((0, 16), (1, 16))),
        "momentum": normal_values(splits[6], (COLS, D), 0.5, 6.0, ((0, 16),)),
        "tile_lists": draw_tile_lists(jax.random.fold_in(splits[8], 71), 0),
    }


def reference(tokens, out_grad, weights, moment_one, moment_two, error_buf, momentum, tile_lists):
    col_blocks = COLS_DEV // TILE
    feat_blocks = D // TILE
    tile_grid = jnp.arange(TILES_DEV, dtype=jnp.int32)
    corr_one = 1.0 - 0.8 ** 20
    corr_two = 1.0 - 0.99 ** 20
    summed = jnp.zeros((COLS, D), jnp.float32)
    errors = []
    for replica in range(REPS):
        gradient = jnp.dot(out_grad[replica].T, tokens[replica], preferred_element_type=jnp.float32)
        first = 0.8 * moment_one[replica].astype(jnp.float32) + 0.2 * gradient
        second = 0.99 * moment_two[replica].astype(jnp.float32) + 0.01 * gradient * gradient
        delta = 0.5 * (first / corr_one / (jnp.sqrt(second / corr_two) + 1e-08) + 0.1 * weights)
        accrued = 0.95 * error_buf[replica].astype(jnp.float32) + delta
        listed = tile_lists[replica]
        chosen = jnp.any(listed[:, :, None] == tile_grid[None, None, :], axis=1)
        chosen = chosen.reshape(N_TP, col_blocks, 1, feat_blocks, 1)
        tile_mask = jnp.broadcast_to(chosen, (N_TP, col_blocks, TILE, feat_blocks, TILE)).reshape(COLS, D)
        rounded = accrued.astype(jnp.bfloat16).astype(jnp.float32)
        summed = summed + jnp.where(tile_mask, rounded, 0.0)
        errors.append(jnp.where(tile_mask, 0.0, accrued).astype(jnp.bfloat16))
    aggregate = summed / REPS
    velocity = 0.9 * momentum.astype(jnp.float32) + aggregate
    weights_new = weights - 0.7 * (aggregate + 0.9 * velocity)
    return (weights_new, jnp.stack(errors), velocity.astype(jnp.bfloat16))
```

```python
import functools

import jax
import jax.numpy as jnp
from jax import lax
from jax.experimental import pallas as pl
from jax.experimental.pallas import tpu as pltpu
from jax.sharding import PartitionSpec as P

N = 4
ROWS = 192
HALF = 2048
COLS = 128
TILE = 128
FEATS = 4096
SLOTS = 4
PIECE = SLOTS * 64 + 16
BF = jnp.bfloat16
F32 = jnp.float32
VMEM_CAP = 40 * 1024 * 1024


def along_x(v, s):
    return lax.ppermute(v, "tp", [(N * a + b, N * ((a + s) % N) + b) for a in range(N) for b in range(N)])


def along_y(v, s):
    return lax.ppermute(v, "tp", [(N * a + b, N * a + (b + s) % N) for a in range(N) for b in range(N)])


def along_z(v, s):
    return lax.ppermute(v, "rep", [(2 * a + c, 2 * ((a + s) % 8) + c) for a in range(8) for c in range(2)])


def across(v):
    return lax.ppermute(v, "rep", [(2 * a + c, 2 * a + 1 - c) for a in range(8) for c in range(2)])


def pack(pos, tokens, og4, part, shift):
    alone = part >= 2
    base = 0 if alone else HALF
    by_y = part % 2 == 0

    def kernel(pos_ref, og_ref, *refs):
        out_ref = refs[-1]
        if not alone:
            out_ref[:, 0:HALF] = refs[0][...]
        for i in range(N):
            out_ref[:, base + COLS * i : base + COLS * (i + 1)] = og_ref[i, 0] if by_y else og_ref[0, i]

    if by_y:
        og_spec = pl.BlockSpec((N, 1, ROWS, COLS), lambda i, p: (0, lax.rem(p[1] + shift, N), 0, 0))
    else:
        og_spec = pl.BlockSpec((1, N, ROWS, COLS), lambda i, p: (lax.rem(p[0] + shift, N), 0, 0, 0))
    tok_spec = pl.BlockSpec((ROWS, HALF), lambda i, p: (0, part))
    width = base + N * COLS
    return pl.pallas_call(
        kernel,
        out_shape=jax.ShapeDtypeStruct((ROWS, width), BF),
        grid_spec=pltpu.PrefetchScalarGridSpec(
            num_scalar_prefetch=1,
            grid=(1,),
            in_specs=[og_spec] if alone else [og_spec, tok_spec],
            out_specs=pl.BlockSpec((ROWS, width), lambda i, p: (0, 0)),
        ),
        cost_estimate=pl.CostEstimate(flops=0, bytes_accessed=4 * ROWS * width, transcendentals=0),
        compiler_params=pltpu.CompilerParams(vmem_limit_bytes=VMEM_CAP),
        name="pack",
    )(pos, og4, *([] if alone else [tokens]))


def partials(pos, og4, o_from, tokens, t_from, part):
    near_o, far_o, op_o = o_from
    near_t, far_t, op1, op2 = t_from
    width = 512
    first = part * (HALF // width)

    def kernel(pos_ref, own_o, n_o, f_o, p_o, t, l, r, a, b, out0, out1, out3, out2, lhs, rhs):
        @pl.when(pl.program_id(0) == 0)
        def _():
            here = pos_ref[1 - part]
            for s, d in enumerate((0, N - 1, 1, 2)):
                k = lax.rem(here + d, N)
                rows = pl.ds(ROWS * s, ROWS)
                lhs[rows, 0:COLS] = own_o[0, k] if part == 0 else own_o[k, 0]
                lanes = pl.ds(pl.multiple_of(k * COLS, COLS), COLS)
                lhs[rows, COLS : 2 * COLS] = n_o[:, lanes]
                lhs[rows, 2 * COLS : 3 * COLS] = f_o[:, lanes]
                lhs[rows, 3 * COLS : 4 * COLS] = p_o[:, lanes]

        rhs[0:192] = t[...]
        rhs[192:384] = l[...]
        rhs[384:576] = r[...]
        rhs[576:672] = a[...]
        rhs[672:768] = b[...]
        res = lax.dot_general(lhs[...], rhs[...], (((0,), (0,)), ((), ())), preferred_element_type=F32)
        out0[...] = res[0:COLS]
        out1[...] = res[COLS : 2 * COLS].astype(BF)
        out3[...] = res[2 * COLS : 3 * COLS].astype(BF)
        out2[...] = res[3 * COLS : 4 * COLS].astype(BF)

    own_spec = (
        pl.BlockSpec((1, N, ROWS, COLS), lambda i, p: (p[0], 0, 0, 0))
        if part == 0
        else pl.BlockSpec((N, 1, ROWS, COLS), lambda i, p: (0, p[1], 0, 0))
    )
    tail = pl.BlockSpec((ROWS, 512), lambda i, p: (0, HALF // 512))
    piece = pl.BlockSpec((ROWS, 512), lambda i, p: (0, 0))
    lanes = lambda rows, off=0: pl.BlockSpec((rows, width), lambda i, p: (0, i + off))
    outs = [jax.ShapeDtypeStruct((COLS, HALF), d) for d in (F32, BF, BF, BF)]
    return pl.pallas_call(
        kernel,
        out_shape=outs,
        grid_spec=pltpu.PrefetchScalarGridSpec(
            num_scalar_prefetch=1,
            grid=(HALF // width,),
            in_specs=[own_spec, tail, tail, piece, lanes(ROWS, first), lanes(ROWS), lanes(ROWS), lanes(ROWS // 2), lanes(ROWS // 2)],
            out_specs=[lanes(COLS)] * 4,
            scratch_shapes=[pltpu.VMEM((N * ROWS, N * COLS), BF), pltpu.VMEM((N * ROWS, width), BF)],
        ),
        compiler_params=pltpu.CompilerParams(vmem_limit_bytes=VMEM_CAP),
        cost_estimate=pl.CostEstimate(flops=2 * 768 * 512 * HALF, bytes_accessed=8 << 20, transcendentals=0),
        name="partials",
    )(pos, og4, near_o, far_o, op_o, tokens, near_t, far_t, op1, op2)


def epilogue(ids, pos, grads, m1, m2, err, weights):
    width = 512
    steps = FEATS // width
    half = steps // 2
    corr_one = 1.0 - 0.8**20
    corr_two = 1.0 - 0.99**20

    def kernel(ids_ref, pos_ref, a0, a1, a2, a3, b0, b1, b2, b3, m1_ref, m2_ref, e_ref, w_ref, out, mine, other, grad):
        i = pl.program_id(0)

        @pl.when(i == 0)
        def _():
            row = lax.broadcasted_iota(jnp.int32, (16, TILE), 0)
            v = jnp.full((16, TILE), -1, jnp.int32)
            for k in range(SLOTS):
                v = jnp.where(row == k, ids_ref[k], v)
            v = v.astype(F32).astype(BF)
            for ref in (mine, other):
                ref[0 : SLOTS * 64] = jnp.zeros((SLOTS * 64, TILE), BF)
                ref[SLOTS * 64 :] = v

        @pl.when(i < half)
        def _():
            grad[...] = a0[...] + (a1[...].astype(F32) + a2[...].astype(F32)) + a3[...].astype(F32)

        @pl.when(i >= half)
        def _():
            grad[...] = b0[...] + (b1[...].astype(F32) + b2[...].astype(F32)) + b3[...].astype(F32)

        core = pos_ref[2]
        for j in range(width // TILE):
            at = slice(j * TILE, (j + 1) * TILE)
            g = grad[:, at]
            first = 0.8 * m1_ref[:, at].astype(F32) + 0.2 * g
            second = 0.99 * m2_ref[:, at].astype(F32) + 0.01 * g * g
            delta = 0.5 * (first / corr_one / (jnp.sqrt(second / corr_two) + 1e-08) + 0.1 * w_ref[:, at])
            acc = (0.95 * e_ref[:, at].astype(F32) + delta).astype(BF)
            t = i * (width // TILE) + j
            hit = (ids_ref[0] == t) | (ids_ref[1] == t) | (ids_ref[2] == t) | (ids_ref[3] == t)
            out[:, at] = acc

            @pl.when(hit)
            def _():
                out[:, at] = jnp.zeros((COLS, TILE), BF)
                for k in range(SLOTS):

                    @pl.when(ids_ref[k] == t)
                    def _():
                        top, bottom = acc[0:64], acc[64:128]

                        @pl.when(core == 0)
                        def _():
                            mine[64 * k : 64 * k + 64] = top
                            other[64 * k : 64 * k + 64] = bottom

                        @pl.when(core == 1)
                        def _():
                            mine[64 * k : 64 * k + 64] = bottom
                            other[64 * k : 64 * k + 64] = top

    blk = lambda f: pl.BlockSpec((COLS, width), f)
    a_spec = blk(lambda i, *_: (0, jnp.minimum(i, half - 1)))
    b_spec = blk(lambda i, *_: (0, jnp.maximum(i - half, 0)))
    full = blk(lambda i, *_: (0, i))
    keep = pl.BlockSpec((PIECE, TILE), lambda i, *_: (0, 0))
    return pl.pallas_call(
        kernel,
        out_shape=[
            jax.ShapeDtypeStruct((COLS, FEATS), BF),
            jax.ShapeDtypeStruct((PIECE, TILE), BF),
            jax.ShapeDtypeStruct((PIECE, TILE), BF),
        ],
        grid_spec=pltpu.PrefetchScalarGridSpec(
            num_scalar_prefetch=2,
            grid=(steps,),
            in_specs=[a_spec] * 4 + [b_spec] * 4 + [full] * 4,
            out_specs=[full, keep, keep],
            scratch_shapes=[pltpu.VMEM((COLS, width), F32)],
        ),
        compiler_params=pltpu.CompilerParams(vmem_limit_bytes=VMEM_CAP),
        cost_estimate=pl.CostEstimate(flops=20 * COLS * FEATS, bytes_accessed=10 << 20, transcendentals=0),
        name="epilogue",
    )(ids, pos, *grads, m1, m2, err, weights)


def add_tiles(ids, pieces):
    n = len(pieces)

    def kernel(ids_ref, *refs):
        ins, out, acc = refs[:n], refs[n], refs[n + 1]
        acc[...] = jnp.zeros_like(acc)
        at = 0
        for ref in ins:
            for h in range(ref.shape[0] // PIECE):
                for k in range(SLOTS):
                    t = ids_ref[at]
                    at += 1

                    @pl.when(t >= 0)
                    def _():
                        lanes = pl.ds(pl.multiple_of(t * TILE, TILE), TILE)
                        row = h * PIECE + 64 * k
                        acc[:, lanes] = acc[:, lanes] + ref[row : row + 64].astype(F32)

        out[...] = (acc[...] * (1.0 / 16.0)).astype(BF)

    whole = lambda p: pl.BlockSpec(p.shape, lambda i, *_: (0, 0))
    return pl.pallas_call(
        kernel,
        out_shape=jax.ShapeDtypeStruct((64, FEATS), BF),
        grid_spec=pltpu.PrefetchScalarGridSpec(
            num_scalar_prefetch=1,
            grid=(1,),
            in_specs=[whole(p) for p in pieces],
            out_specs=pl.BlockSpec((64, FEATS), lambda i, *_: (0, 0)),
            scratch_shapes=[pltpu.VMEM((64, FEATS), F32)],
        ),
        compiler_params=pltpu.CompilerParams(vmem_limit_bytes=VMEM_CAP),
        cost_estimate=pl.CostEstimate(flops=64 * 64 * 128, bytes_accessed=3 << 20, transcendentals=0),
        name="add_tiles",
    )(ids, *pieces)


def outer(pos, mine, other, weights, momentum):
    width = 1024

    def kernel(pos_ref, m_ref, o_ref, w_ref, v_ref, w_out, v_out):
        core = pos_ref[2]
        for h in range(2):
            rows = slice(64 * h, 64 * h + 64)
            agg = jnp.where(core == h, m_ref[...].astype(F32), o_ref[...].astype(F32))
            vel = 0.9 * v_ref[rows].astype(F32) + agg
            w_out[rows] = w_ref[rows] - 0.7 * (agg + 0.9 * vel)
            v_out[rows] = vel.astype(BF)

    part = pl.BlockSpec((64, width), lambda i, *_: (0, i))
    full = pl.BlockSpec((COLS, width), lambda i, *_: (0, i))
    return pl.pallas_call(
        kernel,
        out_shape=[jax.ShapeDtypeStruct((COLS, FEATS), F32), jax.ShapeDtypeStruct((COLS, FEATS), BF)],
        grid_spec=pltpu.PrefetchScalarGridSpec(
            num_scalar_prefetch=1,
            grid=(FEATS // width,),
            in_specs=[part, part, full, full],
            out_specs=[full, full],
        ),
        compiler_params=pltpu.CompilerParams(vmem_limit_bytes=VMEM_CAP),
        cost_estimate=pl.CostEstimate(flops=6 * COLS * FEATS, bytes_accessed=8 << 20, transcendentals=0),
        name="outer",
    )(pos, mine, other, weights, momentum)


def per_device(tokens, out_grad, weights, moment_one, moment_two, error_buf, momentum, tile_lists):
    tp = lax.axis_index("tp")
    core = lax.rem(lax.axis_index("rep"), 2)
    pos = jnp.stack([tp // N, lax.rem(tp, N), core]).astype(jnp.int32)
    tok = tokens[0]
    og4 = out_grad[0].reshape(N, N, ROWS, COLS)
    ids = tile_lists[0, 0]

    yp = along_y(pack(pos, tok, og4, 0, 1), 1)
    ym = along_y(pack(pos, tok, og4, 0, 3), 3)
    xp = along_x(pack(pos, tok, og4, 1, 1), 1)
    xm = along_x(pack(pos, tok, og4, 1, 3), 3)
    ox = along_x(pack(pos, tok, og4, 3, 2), 2)
    oy = along_y(pack(pos, tok, og4, 2, 2), 2)
    half = ROWS // 2
    y1 = along_y(yp[:half, :HALF], 1)
    y2 = along_y(ym[half:, :HALF], 3)
    x1 = along_x(xp[:half, :HALF], 1)
    x2 = along_x(xm[half:, :HALF], 3)

    pa = partials(pos, og4, (xp, xm, ox), tok, (yp, ym, y1, y2), 0)
    pb = partials(pos, og4, (yp, ym, oy), tok, (xp, xm, x1, x2), 1)
    ga = [pa[0], along_x(pa[1], 3), along_x(pa[2], 1), along_x(pa[3], 2)]
    gb = [pb[0], along_y(pb[1], 3), along_y(pb[2], 1), along_y(pb[3], 2)]

    error_new, mine, other = epilogue(ids, pos, ga + gb, moment_one[0], moment_two[0], error_buf[0], weights)

    own = jnp.concatenate([mine, across(other)])
    u1, d1 = along_z(own, 1), along_z(own, 7)
    u2, d2 = along_z(u1, 1), along_z(d1, 7)
    u3, d3 = along_z(u2, 1), along_z(d2, 7)
    u4, d4 = along_z(u3[:PIECE], 1), along_z(d3[PIECE:], 7)
    pieces = [own, u1, d1, u2, d2, u3, d3, u4, d4]
    got = [p.reshape(-1, PIECE, TILE)[:, SLOTS * 64 : SLOTS * 64 + SLOTS, 0] for p in pieces]
    got = jnp.concatenate(got).astype(jnp.int32).reshape(-1)
    agg = add_tiles(got, pieces)
    weights_new, momentum_new = outer(pos, agg, across(agg), weights, momentum)
    return (weights_new, error_new[None], momentum_new)


def solution(mesh):
    return jax.shard_map(
        per_device,
        mesh=mesh,
        in_specs=(
            P("rep", "tp", None),
            P("rep", None, "tp"),
            P("tp", None),
            P("rep", "tp", None),
            P("rep", "tp", None),
            P("rep", "tp", None),
            P("tp", None),
            P("rep", "tp", None),
        ),
        out_specs=(P("tp", None), P("rep", "tp", None), P("tp", None)),
        check_vma=False,
    )
```

```python
import functools

import jax
import jax.numpy as jnp
from jax import lax
from jax.experimental import pallas as pl
from jax.experimental.pallas import tpu as pltpu
from jax.sharding import PartitionSpec as P

N = 4
ROWS = 192
HALF = 2048
COLS = 128
TILE = 128
FEATS = 4096
SLOTS = 4
PIECE = SLOTS * COLS + 16
T_ROWS = HALF // TILE * ROWS
O_ROWS = N * ROWS
IDS = 16
FIRST = T_ROWS + O_ROWS + O_ROWS // 2 + IDS
RELAY = T_ROWS // 2 + O_ROWS // 2 + IDS
BF = jnp.bfloat16
F32 = jnp.float32
SMALL_CAP = 8 * 1024 * 1024
PACK_CAP = 50 * 1024 * 1024
VMEM = pl.BlockSpec(memory_space=pltpu.VMEM)


def along_x(v, s):
    return lax.ppermute(v, "tp", [(N * a + b, N * ((a + s) % N) + b) for a in range(N) for b in range(N)])


def along_y(v, s):
    return lax.ppermute(v, "tp", [(N * a + b, N * a + (b + s) % N) for a in range(N) for b in range(N)])


def onward(v):
    pairs = [(2 * a, 2 * ((a + 1) % 8)) for a in range(8)] + [(2 * a + 1, 2 * ((a + 7) % 8) + 1) for a in range(8)]
    return lax.ppermute(v, "rep", pairs)


def across(v):
    return lax.ppermute(v, "rep", [(2 * a + c, 2 * a + 1 - c) for a in range(8) for c in range(2)])


def put_ids(ref, row, read):
    at = lax.broadcasted_iota(jnp.int32, (IDS, TILE), 0)
    v = jnp.zeros((IDS, TILE), jnp.int32)
    for k in range(SLOTS):
        v = jnp.where(at == k, read(k) + 1, v)
    ref[row : row + IDS] = v.astype(F32).astype(BF)


def get_ids(block):
    at = lax.broadcasted_iota(jnp.int32, (IDS, TILE), 0)
    lane = lax.broadcasted_iota(jnp.int32, (IDS, TILE), 1)
    scale = jnp.where(at == 0, 1.0, jnp.where(at == 1, 64.0, jnp.where(at == 2, 4096.0, 262144.0)))
    scale = jnp.where((lane == 0) & (at < SLOTS), scale, 0.0)
    code = jnp.sum(block.astype(F32) * scale).astype(jnp.int32)
    return [((code >> (6 * k)) & 63) - 1 for k in range(SLOTS)]


def pack(pos, lists, tokens, og4):
    def kernel(pos_ref, ids_hbm, tok_hbm, og_hbm, *rest):
        outs, (ids, tok, near, far, sems) = rest[:4], rest[4:]
        x, y = pos_ref[0], pos_ref[1]
        copies = [
            pltpu.make_async_copy(ids_hbm, ids, sems.at[0]),
            pltpu.make_async_copy(tok_hbm.at[:, pl.ds(0, HALF)], tok.at[0], sems.at[1]),
            pltpu.make_async_copy(og_hbm.at[:, lax.rem(y + 1, N)], near.at[0], sems.at[2]),
            pltpu.make_async_copy(og_hbm.at[:, lax.rem(y + 3, N)], near.at[1], sems.at[3]),
            pltpu.make_async_copy(og_hbm.at[:, lax.rem(y + 2, N)], far.at[0], sems.at[4]),
            pltpu.make_async_copy(tok_hbm.at[:, pl.ds(HALF, HALF)], tok.at[1], sems.at[5]),
            pltpu.make_async_copy(og_hbm.at[lax.rem(x + 1, N)], near.at[2], sems.at[6]),
            pltpu.make_async_copy(og_hbm.at[lax.rem(x + 3, N)], near.at[3], sems.at[7]),
            pltpu.make_async_copy(og_hbm.at[lax.rem(x + 2, N)], far.at[1], sems.at[8]),
        ]
        for c in copies:
            c.start()
        copies[0].wait()
        for out in outs:
            put_ids(out, FIRST - IDS, lambda k: ids[0, k])
        for part in range(2):
            for c in copies[1 + 4 * part : 5 + 4 * part]:
                c.wait()
            for way in range(2):
                out = outs[2 * part + way]
                for j in range(HALF // TILE):
                    out[ROWS * j : ROWS * (j + 1)] = tok[part, :, TILE * j : TILE * (j + 1)]
                for i in range(N):
                    row = T_ROWS + ROWS * i
                    out[row : row + ROWS] = near[2 * part + way, i]
                for i in range(2):
                    row = T_ROWS + O_ROWS + ROWS * i
                    out[row : row + ROWS] = far[part, 2 * way + i]

    hbm = pl.BlockSpec(memory_space=pltpu.HBM)
    return pl.pallas_call(
        kernel,
        out_shape=[jax.ShapeDtypeStruct((FIRST, TILE), BF)] * 4,
        in_specs=[pl.BlockSpec(memory_space=pltpu.SMEM), hbm, hbm, hbm],
        out_specs=[VMEM] * 4,
        scratch_shapes=[
            pltpu.SMEM((1, SLOTS), jnp.int32),
            pltpu.VMEM((2, ROWS, HALF), BF),
            pltpu.VMEM((4, N, ROWS, COLS), BF),
            pltpu.VMEM((2, N, ROWS, COLS), BF),
            pltpu.SemaphoreType.DMA((9,)),
        ],
        cost_estimate=pl.CostEstimate(flops=0, bytes_accessed=16 * FIRST * TILE, transcendentals=0),
        compiler_params=pltpu.CompilerParams(vmem_limit_bytes=PACK_CAP),
        name="pack",
    )(pos, lists, tokens, og4)


def relay(message, shift):
    lo = 0 if shift == 1 else ROWS // 2
    hi = lo + ROWS // 2

    def kernel(ref, out):
        for j in range(HALF // TILE):
            out[ROWS // 2 * j : ROWS // 2 * (j + 1)] = ref[ROWS * j + lo : ROWS * j + hi]
        out[T_ROWS // 2 :] = ref[T_ROWS + O_ROWS :]

    return pl.pallas_call(
        kernel,
        out_shape=jax.ShapeDtypeStruct((RELAY, TILE), BF),
        in_specs=[VMEM],
        out_specs=VMEM,
        compiler_params=pltpu.CompilerParams(vmem_limit_bytes=SMALL_CAP),
        cost_estimate=pl.CostEstimate(flops=0, bytes_accessed=4 * RELAY * TILE, transcendentals=0),
        name="relay",
    )(message)


def gather(pos, ids, og4, near_o, far_o, tokens, near_t, far_t, part):
    def kernel(pos_ref, ids_ref, own_o, n_o, f_o, t, l, r, rhs, turned, listed, lhs):
        x, y = pos_ref[0], pos_ref[1]
        here = pos_ref[1 - part]
        for s, d in enumerate((0, N - 1, 1, 2)):
            k = lax.rem(here + d, N)
            rows = slice(ROWS * s, ROWS * (s + 1))
            their = pl.ds(pl.multiple_of(T_ROWS + k * ROWS, ROWS), ROWS)
            lhs[rows, 0:COLS] = own_o[x, k] if part == 0 else own_o[k, y]
            lhs[rows, COLS : 2 * COLS] = n_o[their]
            lhs[rows, 2 * COLS : 3 * COLS] = f_o[their]
        for p in range(3):
            at = slice(COLS * p, COLS * (p + 1))
            turned[at] = lhs[:, at].T
        for p, ref in enumerate((None, n_o, f_o)):
            found = [ids_ref[k] for k in range(SLOTS)] if ref is None else get_ids(ref[FIRST - IDS :])
            for k in range(SLOTS):
                listed[SLOTS * p + k] = found[k] - part * (HALF // TILE)
        rhs[0:ROWS] = t[:, HALF * part : HALF * (part + 1)]
        for j in range(HALF // TILE):
            at = slice(TILE * j, TILE * (j + 1))
            rows = slice(ROWS * j, ROWS * (j + 1))
            rhs[ROWS : 2 * ROWS, at] = l[rows]
            rhs[2 * ROWS : 3 * ROWS, at] = r[rows]

    smem = pl.BlockSpec(memory_space=pltpu.SMEM)
    return pl.pallas_call(
        kernel,
        out_shape=[
            jax.ShapeDtypeStruct((N * ROWS, HALF), BF),
            jax.ShapeDtypeStruct((N * COLS, N * ROWS), BF),
            jax.ShapeDtypeStruct((N * SLOTS,), jnp.int32),
        ],
        in_specs=[smem, smem] + [VMEM] * 6,
        out_specs=[VMEM, VMEM, smem],
        scratch_shapes=[pltpu.VMEM((N * ROWS, 3 * COLS), BF)],
        compiler_params=pltpu.CompilerParams(vmem_limit_bytes=SMALL_CAP),
        cost_estimate=pl.CostEstimate(flops=0, bytes_accessed=8 << 20, transcendentals=0),
        name="gather",
    )(pos, ids, og4, near_o, far_o, tokens, near_t, far_t)


def partials(pos, ready, lo_o, hi_o, op1, op2, part, *after):
    width = 512
    half = ROWS // 2
    tiles = HALF // TILE

    def kernel(pos_ref, listed, lo, hi, a, b, rhs_in, turned_in, *rest):
        own, near, far, own_sel, to_near, to_far, op_sel, rhs, turned, lhs, op, beyond, found = rest[len(after) :]
        op[0 : O_ROWS // 2] = lo[T_ROWS // 2 : T_ROWS // 2 + O_ROWS // 2]
        op[O_ROWS // 2 :] = hi[T_ROWS // 2 : T_ROWS // 2 + O_ROWS // 2]
        here = pos_ref[1 - part]
        for s, d in enumerate((0, N - 1, 1, 2)):
            k = lax.rem(here + d, N)
            lhs[ROWS * s : ROWS * (s + 1)] = op[pl.ds(pl.multiple_of(k * ROWS, ROWS), ROWS)]
        turned[3 * COLS :] = lhs[...].T
        for k in range(3 * SLOTS):
            found[k] = listed[k]
        for k, t in enumerate(get_ids(lo[RELAY - IDS :])):
            found[3 * SLOTS + k] = t - part * tiles
        for j in range(tiles):
            at = slice(TILE * j, TILE * (j + 1))
            rhs[3 * ROWS : 3 * ROWS + half, at] = a[half * j : half * (j + 1)]
            rhs[3 * ROWS + half :, at] = b[half * j : half * (j + 1)]
        for i in range(HALF // width):
            at = slice(width * i, width * (i + 1))
            res = jnp.dot(turned[...], rhs[:, at], preferred_element_type=F32)
            own[:, at] = res[0:COLS]
            near[:, at] = res[COLS : 2 * COLS].astype(BF)
            far[:, at] = res[2 * COLS : 3 * COLS].astype(BF)
            beyond[:, at] = res[3 * COLS :].astype(BF)
        for j in range(tiles):
            out = to_far if j < tiles // 2 else to_near
            row = SLOTS * COLS + COLS * (j % (tiles // 2))
            out[row : row + COLS] = beyond[:, TILE * j : TILE * (j + 1)]
        for p, (out, sel) in enumerate(((own, own_sel), (near, to_near), (far, to_far), (beyond, op_sel))):
            for k in range(SLOTS):
                t = found[SLOTS * p + k]

                @pl.when((t >= 0) & (t < tiles))
                def _():
                    sel[COLS * k : COLS * (k + 1)] = out[:, pl.ds(pl.multiple_of(t * TILE, TILE), TILE)]

    smem = pl.BlockSpec(memory_space=pltpu.SMEM)
    rhs, turned, listed = ready
    shape = jax.ShapeDtypeStruct
    wide, message, few = (COLS, HALF), (SLOTS * COLS + COLS * tiles // 2, TILE), (SLOTS * COLS, TILE)
    return pl.pallas_call(
        kernel,
        out_shape=[shape(wide, F32), shape(wide, BF), shape(wide, BF), shape(few, F32), shape(message, BF), shape(message, BF), shape(few, BF)]
        + [shape(v.shape, v.dtype) for v in (rhs, turned)],
        in_specs=[smem, smem] + [VMEM] * 6 + [pl.BlockSpec(memory_space=pl.ANY)] * len(after),
        out_specs=[VMEM] * 9,
        input_output_aliases={6: 7, 7: 8},
        scratch_shapes=[
            pltpu.VMEM((N * ROWS, COLS), BF),
            pltpu.VMEM((O_ROWS, TILE), BF),
            pltpu.VMEM(wide, BF),
            pltpu.SMEM((N * SLOTS,), jnp.int32),
        ],
        compiler_params=pltpu.CompilerParams(vmem_limit_bytes=SMALL_CAP),
        cost_estimate=pl.CostEstimate(flops=2 * 768 * 512 * HALF, bytes_accessed=8 << 20, transcendentals=0),
        name="partials",
    )(pos, listed, lo_o, hi_o, op1, op2, rhs, turned, *after)


def add_beyond(near, far, from_near, from_far):
    tiles = HALF // TILE // 2

    def kernel(near_in, far_in, a, b, near_ref, far_ref):
        for j in range(tiles):
            rows = slice(SLOTS * COLS + COLS * j, SLOTS * COLS + COLS * (j + 1))
            lo = slice(TILE * j, TILE * (j + 1))
            hi = slice(HALF // 2 + TILE * j, HALF // 2 + TILE * (j + 1))
            far_ref[:, lo] = (far_in[:, lo].astype(F32) + a[rows].astype(F32)).astype(BF)
            near_ref[:, hi] = (near_in[:, hi].astype(F32) + b[rows].astype(F32)).astype(BF)

    return pl.pallas_call(
        kernel,
        out_shape=[jax.ShapeDtypeStruct((COLS, HALF), BF)] * 2,
        in_specs=[VMEM] * 4,
        out_specs=[VMEM] * 2,
        input_output_aliases={0: 0, 1: 1},
        compiler_params=pltpu.CompilerParams(vmem_limit_bytes=SMALL_CAP),
        cost_estimate=pl.CostEstimate(flops=COLS * HALF, bytes_accessed=3 << 20, transcendentals=0),
        name="add_beyond",
    )(near, far, from_near, from_far)


CORR_ONE = 1.0 - 0.8**20
CORR_TWO = 1.0 - 0.99**20


def accrue(g, m1, m2, e, w):
    top = (0.4 / CORR_ONE) * m1.astype(F32) + (0.1 / CORR_ONE) * g
    v = (0.99 / CORR_TWO) * m2.astype(F32) + (0.01 / CORR_TWO) * (g * g)
    low = v * lax.rsqrt(v) + 1e-08
    near = pltpu.reciprocal(low, approx=True)
    delta = top * (near * (2.0 - low * near)) + 0.05 * w
    return (0.95 * e.astype(F32) + delta).astype(BF)


def total(refs):
    return refs[0][...] + functools.reduce(jnp.add, [r[...].astype(F32) for r in refs[1:]])


def sent_tiles(ids, sels, m1, m2, err, weights):
    def kernel(ids_ref, *refs):
        a, b = refs[0:4], refs[4:8]
        m1_ref, m2_ref, e_ref, w_ref, out, grad = refs[8:]
        put_ids(out, SLOTS * COLS, lambda s: ids_ref[s])
        for k in range(SLOTS):
            t = ids_ref[k]
            rows = slice(COLS * k, COLS * (k + 1))

            @pl.when(t < 0)
            def _():
                out[rows] = jnp.zeros((COLS, TILE), BF)

            @pl.when(t >= 0)
            def _():
                @pl.when(t < HALF // TILE)
                def _():
                    grad[...] = total([r.at[rows] for r in a])

                @pl.when(t >= HALF // TILE)
                def _():
                    grad[...] = total([r.at[rows] for r in b])

                at = pl.ds(pl.multiple_of(t * TILE, TILE), TILE)
                out[rows] = accrue(grad[...], m1_ref[:, at], m2_ref[:, at], e_ref[:, at], w_ref[:, at])

    return pl.pallas_call(
        kernel,
        out_shape=jax.ShapeDtypeStruct((PIECE, TILE), BF),
        in_specs=[pl.BlockSpec(memory_space=pltpu.SMEM)] + [VMEM] * 12,
        out_specs=VMEM,
        scratch_shapes=[pltpu.VMEM((COLS, TILE), F32)],
        compiler_params=pltpu.CompilerParams(vmem_limit_bytes=SMALL_CAP),
        cost_estimate=pl.CostEstimate(flops=20 * SLOTS * COLS * TILE, bytes_accessed=2 << 20, transcendentals=0),
        name="sent_tiles",
    )(ids, *sels, m1, m2, err, weights)


def tied(vs, after):
    n = len(vs)
    return pl.pallas_call(
        lambda *refs: None,
        out_shape=[jax.ShapeDtypeStruct(v.shape, v.dtype) for v in vs],
        in_specs=[pl.BlockSpec(memory_space=pl.ANY)] * (n + len(after)),
        out_specs=[pl.BlockSpec(memory_space=pl.ANY)] * n,
        input_output_aliases={i: i for i in range(n)},
        compiler_params=pltpu.CompilerParams(vmem_limit_bytes=SMALL_CAP),
        cost_estimate=pl.CostEstimate(flops=0, bytes_accessed=0, transcendentals=0),
        name="tied",
    )(*vs, *after)


def pair(mine, other, *after):
    def kernel(a, b, *rest):
        rest[-1][0:PIECE] = a[...]
        rest[-1][PIECE:] = b[...]

    return pl.pallas_call(
        kernel,
        out_shape=jax.ShapeDtypeStruct((2 * PIECE, TILE), BF),
        in_specs=[VMEM] * 2 + [pl.BlockSpec(memory_space=pl.ANY)] * len(after),
        out_specs=VMEM,
        compiler_params=pltpu.CompilerParams(vmem_limit_bytes=SMALL_CAP),
        cost_estimate=pl.CostEstimate(flops=0, bytes_accessed=8 * PIECE * TILE, transcendentals=0),
        name="pair",
    )(mine, other, *after)


def own_half(both, *after):
    def kernel(ref, *rest):
        rest[-1][...] = ref[0:PIECE]

    return pl.pallas_call(
        kernel,
        out_shape=jax.ShapeDtypeStruct((PIECE, TILE), BF),
        in_specs=[VMEM] + [pl.BlockSpec(memory_space=pl.ANY)] * len(after),
        out_specs=VMEM,
        compiler_params=pltpu.CompilerParams(vmem_limit_bytes=SMALL_CAP),
        cost_estimate=pl.CostEstimate(flops=0, bytes_accessed=4 * PIECE * TILE, transcendentals=0),
        name="own_half",
    )(both, *after)


def keep_error(ids, grads, m1, m2, err, weights, part, before=None):
    width = 512
    tiles = width // TILE
    steps = HALF // width

    def kernel(ids_ref, g0, g1, g2, m1_ref, m2_ref, e_ref, w_ref, *rest):
        out, flag, kept, sems = rest[-4:]
        flag[...] = jnp.zeros_like(flag)
        copies = []
        for i in range(steps):
            for j in range(tiles):
                at = slice(width * i + TILE * j, width * i + TILE * (j + 1))
                to = slice(part * HALF + at.start, part * HALF + at.stop)
                g = total([r.at[:, at] for r in (g0, g1, g2)])
                kept[:, at] = accrue(g, m1_ref[:, to], m2_ref[:, to], e_ref[:, to], w_ref[:, to])
            for k in range(SLOTS):
                j = ids_ref[k] - part * (HALF // TILE) - i * tiles

                @pl.when((j >= 0) & (j < tiles))
                def _():
                    kept[:, pl.ds(pl.multiple_of(width * i + j * TILE, TILE), TILE)] = jnp.zeros((COLS, TILE), BF)

            copies.append(
                pltpu.make_async_copy(
                    kept.at[:, pl.ds(width * i, width)],
                    out.at[:, pl.ds(part * HALF + width * i, width)],
                    sems.at[i],
                )
            )
            copies[-1].start()
        for c in copies:
            c.wait()

    hbm = pl.BlockSpec(memory_space=pltpu.HBM)
    more = [] if before is None else [before]
    return pl.pallas_call(
        kernel,
        out_shape=[jax.ShapeDtypeStruct((COLS, FEATS), BF), jax.ShapeDtypeStruct((8, TILE), F32)],
        in_specs=[pl.BlockSpec(memory_space=pltpu.SMEM)] + [VMEM] * 7 + [hbm] * len(more),
        out_specs=[hbm, VMEM],
        input_output_aliases={8: 0} if more else {},
        scratch_shapes=[pltpu.VMEM((COLS, HALF), BF), pltpu.SemaphoreType.DMA((steps,))],
        compiler_params=pltpu.CompilerParams(vmem_limit_bytes=SMALL_CAP),
        cost_estimate=pl.CostEstimate(flops=20 * COLS * HALF, bytes_accessed=5 << 20, transcendentals=0),
        name="keep_error",
    )(ids, *grads, m1, m2, err, weights, *more)


def add_tiles(pieces, after):
    n = len(pieces)
    halves = sum(p.shape[0] // PIECE for p in pieces)

    def kernel(*refs):
        ins, (out, acc, listed) = refs[:n], refs[-3:]
        where = [(ref, h * PIECE) for ref in ins for h in range(ref.shape[0] // PIECE)]
        for at, (ref, row) in enumerate(where):
            for k, t in enumerate(get_ids(ref[row + SLOTS * COLS : row + PIECE])):
                listed[SLOTS * at + k] = t
        acc[...] = jnp.zeros_like(acc)
        for at, (ref, row) in enumerate(where):
            for k in range(SLOTS):
                t = listed[SLOTS * at + k]

                @pl.when(t >= 0)
                def _():
                    lanes = pl.ds(pl.multiple_of(t * TILE, TILE), TILE)
                    begin = row + COLS * k
                    acc[:, lanes] = acc[:, lanes] + ref[begin : begin + COLS].astype(F32)

        out[...] = (acc[...] * (1.0 / 16.0)).astype(BF)

    return pl.pallas_call(
        kernel,
        out_shape=jax.ShapeDtypeStruct((COLS, FEATS), BF),
        in_specs=[VMEM] * n + [pl.BlockSpec(memory_space=pl.ANY)] * len(after),
        scratch_shapes=[pltpu.VMEM((COLS, FEATS), F32), pltpu.SMEM((halves * SLOTS,), jnp.int32)],
        compiler_params=pltpu.CompilerParams(vmem_limit_bytes=SMALL_CAP),
        cost_estimate=pl.CostEstimate(flops=64 * 64 * 128, bytes_accessed=3 << 20, transcendentals=0),
        name="add_tiles",
    )(*pieces, *after)


def outer(mine, other, weights, momentum):
    width = 512
    steps = FEATS // width

    def kernel(m_ref, o_ref, w_ref, v_ref, w_out, v_out, w_new, v_new, sems):
        copies = []
        for i in range(steps):
            at = slice(width * i, width * (i + 1))
            agg = m_ref[:, at].astype(F32) + o_ref[:, at].astype(F32)
            vel = 0.9 * v_ref[:, at].astype(F32) + agg
            w_new[:, at] = w_ref[:, at] - 0.7 * (agg + 0.9 * vel)
            v_new[:, at] = vel.astype(BF)
            lanes = pl.ds(width * i, width)
            copies.append(pltpu.make_async_copy(w_new.at[:, lanes], w_out.at[:, lanes], sems.at[0, i]))
            copies.append(pltpu.make_async_copy(v_new.at[:, lanes], v_out.at[:, lanes], sems.at[1, i]))
            copies[-2].start()
            copies[-1].start()
        for c in copies:
            c.wait()

    hbm = pl.BlockSpec(memory_space=pltpu.HBM)
    return pl.pallas_call(
        kernel,
        out_shape=[jax.ShapeDtypeStruct((COLS, FEATS), F32), jax.ShapeDtypeStruct((COLS, FEATS), BF)],
        in_specs=[VMEM] * 4,
        out_specs=[hbm, hbm],
        scratch_shapes=[pltpu.VMEM((COLS, FEATS), F32), pltpu.VMEM((COLS, FEATS), BF), pltpu.SemaphoreType.DMA((2, steps))],
        compiler_params=pltpu.CompilerParams(vmem_limit_bytes=SMALL_CAP),
        cost_estimate=pl.CostEstimate(flops=6 * COLS * FEATS, bytes_accessed=8 << 20, transcendentals=0),
        name="outer",
    )(mine, other, weights, momentum)


def per_device(tokens, out_grad, weights, moment_one, moment_two, error_buf, momentum, tile_lists):
    tp = lax.axis_index("tp")
    pos = jnp.stack([tp // N, lax.rem(tp, N)]).astype(jnp.int32)
    tok = tokens[0]
    og4 = out_grad[0].reshape(N, N, ROWS, COLS)
    ids = tile_lists[0, 0]
    state = (moment_one[0], moment_two[0], error_buf[0], weights)

    m = pack(pos, tile_lists[0], tok, og4)
    yp, ym, xp, xm = along_y(m[0], 1), along_y(m[1], 3), along_x(m[2], 1), along_x(m[3], 3)
    y1, y2 = along_y(relay(yp, 1), 1), along_y(relay(ym, 3), 3)
    x1, x2 = along_x(relay(xp, 1), 1), along_x(relay(xm, 3), 3)

    ra = gather(pos, ids, og4, xp, xm, tok, yp, ym, 0)
    rb = gather(pos, ids, og4, yp, ym, tok, xp, xm, 1)
    pa = partials(pos, ra, x1, x2, y1, y2, 0, rb[1])
    sa = [pa[3], along_x(pa[5], 1), along_x(pa[4], 3), along_x(pa[6], 2)]
    pb = partials(pos, rb, y1, y2, x1, x2, 1, pa[3])
    sb = [pb[3], along_y(pb[5], 1), along_y(pb[4], 3), along_y(pb[6], 2)]
    near_a, far_a = add_beyond(pa[1], pa[2], sa[1], sa[2])
    near_b, far_b = add_beyond(pb[1], pb[2], sb[1], sb[2])
    ga = [pa[0], along_x(far_a, 1), along_x(near_a, 3)]
    gb = [pb[0], along_y(far_b, 1), along_y(near_b, 3)]

    mine = sent_tiles(ids, sa + sb, *state)
    own = pair(mine, across(mine))
    (z1,) = tied([onward(own)], ga[1:] + gb[1:])
    z2 = onward(z1)
    z3 = onward(z2)
    error_new, flag = keep_error(ids, ga, *state, 0)
    z4 = onward(own_half(z3, flag))
    error_new, flag = keep_error(ids, gb, *state, 1, error_new)
    agg = add_tiles([mine, z1, z2, z3, z4], [flag])
    weights_new, momentum_new = outer(agg, across(agg), weights, momentum)

    return (weights_new, error_new[None], momentum_new)


def solution(mesh):
    return jax.shard_map(
        per_device,
        mesh=mesh,
        in_specs=(
            P("rep", "tp", None),
            P("rep", None, "tp"),
            P("tp", None),
            P("rep", "tp", None),
            P("rep", "tp", None),
            P("rep", "tp", None),
            P("tp", None),
            P("rep", "tp", None),
        ),
        out_specs=(P("tp", None), P("rep", "tp", None), P("tp", None)),
        check_vma=False,
    )
```

```python
import functools

import jax
import jax.numpy as jnp
from jax import lax
from jax.experimental import pallas as pl
from jax.experimental.pallas import tpu as pltpu
from jax.sharding import PartitionSpec as P

N = 4
ROWS = 192
HALF = 2048
COLS = 128
TILE = 128
FEATS = 4096
SLOTS = 4
PIECE = SLOTS * COLS + 16
T_ROWS = HALF // TILE * ROWS
O_ROWS = N * ROWS
IDS = 16
FIRST = T_ROWS + O_ROWS + O_ROWS // 2 + IDS
RELAY = T_ROWS // 2 + O_ROWS // 2 + IDS
BF = jnp.bfloat16
F32 = jnp.float32
SMALL_CAP = 8 * 1024 * 1024
VMEM = pl.BlockSpec(memory_space=pltpu.VMEM)


def along_x(v, s):
    return lax.ppermute(v, "tp", [(N * a + b, N * ((a + s) % N) + b) for a in range(N) for b in range(N)])


def along_y(v, s):
    return lax.ppermute(v, "tp", [(N * a + b, N * a + (b + s) % N) for a in range(N) for b in range(N)])


def onward(v, s):
    pairs = [(2 * a, 2 * ((a + s) % 8)) for a in range(8)] + [(2 * a + 1, 2 * ((a + 8 - s) % 8) + 1) for a in range(8)]
    return lax.ppermute(v, "rep", pairs)


def across(v):
    return lax.ppermute(v, "rep", [(2 * a + c, 2 * a + 1 - c) for a in range(8) for c in range(2)])


def put_ids(ref, row, read):
    at = lax.broadcasted_iota(jnp.int32, (IDS, TILE), 0)
    v = jnp.zeros((IDS, TILE), jnp.int32)
    for k in range(SLOTS):
        v = jnp.where(at == k, read(k) + 1, v)
    ref[row : row + IDS] = v.astype(F32).astype(BF)


def get_ids(block):
    at = lax.broadcasted_iota(jnp.int32, (IDS, TILE), 0)
    lane = lax.broadcasted_iota(jnp.int32, (IDS, TILE), 1)
    scale = jnp.where(at == 0, 1.0, jnp.where(at == 1, 64.0, jnp.where(at == 2, 4096.0, 262144.0)))
    scale = jnp.where((lane == 0) & (at < SLOTS), scale, 0.0)
    code = jnp.sum(block.astype(F32) * scale).astype(jnp.int32)
    return [((code >> (6 * k)) & 63) - 1 for k in range(SLOTS)]


def pack(place, tokens, og4):
    routes = [(0, 1), (0, 3), (1, 1), (1, 3)]

    def kernel(place_ref, tok, og, *outs):
        for out, (part, shift) in zip(outs, routes, strict=True):
            here = place_ref[1 - part]
            near, far = lax.rem(here + shift, N), lax.rem(here + 2, N)
            lo = 0 if shift == 1 else 2
            for j in range(HALF // TILE):
                out[ROWS * j : ROWS * (j + 1)] = tok[:, HALF * part + TILE * j : HALF * part + TILE * (j + 1)]
            for i in range(N + 2):
                k, other = (i, near) if i < N else (lo + i - N, far)
                row = T_ROWS + ROWS * i
                out[row : row + ROWS] = og[k, other] if part == 0 else og[other, k]
            put_ids(out, FIRST - IDS, lambda k: place_ref[2 + k])

    return pl.pallas_call(
        kernel,
        out_shape=[jax.ShapeDtypeStruct((FIRST, TILE), BF)] * 4,
        in_specs=[pl.BlockSpec(memory_space=pltpu.SMEM), VMEM, VMEM],
        out_specs=[VMEM] * 4,
        cost_estimate=pl.CostEstimate(flops=0, bytes_accessed=16 * FIRST * TILE, transcendentals=0),
        compiler_params=pltpu.CompilerParams(vmem_limit_bytes=SMALL_CAP),
        name="pack",
    )(place, tokens, og4)


def relay(message, shift):
    lo = 0 if shift == 1 else ROWS // 2
    hi = lo + ROWS // 2

    def kernel(ref, out):
        for j in range(HALF // TILE):
            out[ROWS // 2 * j : ROWS // 2 * (j + 1)] = ref[ROWS * j + lo : ROWS * j + hi]
        out[T_ROWS // 2 :] = ref[T_ROWS + O_ROWS :]

    return pl.pallas_call(
        kernel,
        out_shape=jax.ShapeDtypeStruct((RELAY, TILE), BF),
        in_specs=[VMEM],
        out_specs=VMEM,
        compiler_params=pltpu.CompilerParams(vmem_limit_bytes=SMALL_CAP),
        cost_estimate=pl.CostEstimate(flops=0, bytes_accessed=4 * RELAY * TILE, transcendentals=0),
        name="relay",
    )(message)


def gather(pos, ids, og4, near_o, far_o, tokens, near_t, far_t, part):
    def kernel(pos_ref, ids_ref, own_o, n_o, f_o, t, l, r, rhs, turned, listed, lhs):
        x, y = pos_ref[0], pos_ref[1]
        here = pos_ref[1 - part]
        for s, d in enumerate((0, N - 1, 1, 2)):
            k = lax.rem(here + d, N)
            rows = slice(ROWS * s, ROWS * (s + 1))
            their = pl.ds(pl.multiple_of(T_ROWS + k * ROWS, ROWS), ROWS)
            lhs[rows, 0:COLS] = own_o[x, k] if part == 0 else own_o[k, y]
            lhs[rows, COLS : 2 * COLS] = n_o[their]
            lhs[rows, 2 * COLS : 3 * COLS] = f_o[their]
        for p in range(3):
            at = slice(COLS * p, COLS * (p + 1))
            turned[at] = lhs[:, at].T
        for p, ref in enumerate((None, n_o, f_o)):
            found = [ids_ref[k] for k in range(SLOTS)] if ref is None else get_ids(ref[FIRST - IDS :])
            for k in range(SLOTS):
                listed[SLOTS * p + k] = found[k] - part * (HALF // TILE)
        rhs[0:ROWS] = t[:, HALF * part : HALF * (part + 1)]
        for j in range(HALF // TILE):
            at = slice(TILE * j, TILE * (j + 1))
            rows = slice(ROWS * j, ROWS * (j + 1))
            rhs[ROWS : 2 * ROWS, at] = l[rows]
            rhs[2 * ROWS : 3 * ROWS, at] = r[rows]

    smem = pl.BlockSpec(memory_space=pltpu.SMEM)
    return pl.pallas_call(
        kernel,
        out_shape=[
            jax.ShapeDtypeStruct((N * ROWS, HALF), BF),
            jax.ShapeDtypeStruct((N * COLS, N * ROWS), BF),
            jax.ShapeDtypeStruct((N * SLOTS,), jnp.int32),
        ],
        in_specs=[smem, smem] + [VMEM] * 6,
        out_specs=[VMEM, VMEM, smem],
        scratch_shapes=[pltpu.VMEM((N * ROWS, 3 * COLS), BF)],
        compiler_params=pltpu.CompilerParams(vmem_limit_bytes=SMALL_CAP),
        cost_estimate=pl.CostEstimate(flops=0, bytes_accessed=8 << 20, transcendentals=0),
        name="gather",
    )(pos, ids, og4, near_o, far_o, tokens, near_t, far_t)


def partials(pos, ready, lo_o, hi_o, op1, op2, part, *after):
    width = 512
    half = ROWS // 2
    tiles = HALF // TILE

    def kernel(pos_ref, listed, lo, hi, a, b, rhs_in, turned_in, *rest):
        own, near, far, own_sel, to_near, to_far, op_sel, rhs, turned, lhs, op, beyond, found = rest[len(after) :]
        op[0 : O_ROWS // 2] = lo[T_ROWS // 2 : T_ROWS // 2 + O_ROWS // 2]
        op[O_ROWS // 2 :] = hi[T_ROWS // 2 : T_ROWS // 2 + O_ROWS // 2]
        here = pos_ref[1 - part]
        for s, d in enumerate((0, N - 1, 1, 2)):
            k = lax.rem(here + d, N)
            lhs[ROWS * s : ROWS * (s + 1)] = op[pl.ds(pl.multiple_of(k * ROWS, ROWS), ROWS)]
        turned[3 * COLS :] = lhs[...].T
        for k in range(3 * SLOTS):
            found[k] = listed[k]
        for k, t in enumerate(get_ids(lo[RELAY - IDS :])):
            found[3 * SLOTS + k] = t - part * tiles
        for j in range(tiles):
            at = slice(TILE * j, TILE * (j + 1))
            rhs[3 * ROWS : 3 * ROWS + half, at] = a[half * j : half * (j + 1)]
            rhs[3 * ROWS + half :, at] = b[half * j : half * (j + 1)]
        for i in range(HALF // width):
            at = slice(width * i, width * (i + 1))
            res = jnp.dot(turned[...], rhs[:, at], preferred_element_type=F32)
            own[:, at] = res[0:COLS]
            near[:, at] = res[COLS : 2 * COLS].astype(BF)
            far[:, at] = res[2 * COLS : 3 * COLS].astype(BF)
            beyond[:, at] = res[3 * COLS :].astype(BF)
        for j in range(tiles):
            out = to_far if j < tiles // 2 else to_near
            row = SLOTS * COLS + COLS * (j % (tiles // 2))
            out[row : row + COLS] = beyond[:, TILE * j : TILE * (j + 1)]
        for p, (out, sel) in enumerate(((own, own_sel), (near, to_near), (far, to_far), (beyond, op_sel))):
            for k in range(SLOTS):
                t = found[SLOTS * p + k]

                @pl.when((t >= 0) & (t < tiles))
                def _():
                    sel[COLS * k : COLS * (k + 1)] = out[:, pl.ds(pl.multiple_of(t * TILE, TILE), TILE)]

    smem = pl.BlockSpec(memory_space=pltpu.SMEM)
    rhs, turned, listed = ready
    shape = jax.ShapeDtypeStruct
    wide, message, few = (COLS, HALF), (SLOTS * COLS + COLS * tiles // 2, TILE), (SLOTS * COLS, TILE)
    return pl.pallas_call(
        kernel,
        out_shape=[shape(wide, F32), shape(wide, BF), shape(wide, BF), shape(few, F32), shape(message, BF), shape(message, BF), shape(few, BF)]
        + [shape(v.shape, v.dtype) for v in (rhs, turned)],
        in_specs=[smem, smem] + [VMEM] * 6 + [pl.BlockSpec(memory_space=pl.ANY)] * len(after),
        out_specs=[VMEM] * 9,
        input_output_aliases={6: 7, 7: 8},
        scratch_shapes=[
            pltpu.VMEM((N * ROWS, COLS), BF),
            pltpu.VMEM((O_ROWS, TILE), BF),
            pltpu.VMEM(wide, BF),
            pltpu.SMEM((N * SLOTS,), jnp.int32),
        ],
        compiler_params=pltpu.CompilerParams(vmem_limit_bytes=SMALL_CAP),
        cost_estimate=pl.CostEstimate(flops=2 * 768 * 512 * HALF, bytes_accessed=8 << 20, transcendentals=0),
        name="partials",
    )(pos, listed, lo_o, hi_o, op1, op2, rhs, turned, *after)


def add_beyond(near, far, from_near, from_far):
    tiles = HALF // TILE // 2

    def kernel(near_in, far_in, a, b, near_ref, far_ref):
        for j in range(tiles):
            rows = slice(SLOTS * COLS + COLS * j, SLOTS * COLS + COLS * (j + 1))
            lo = slice(TILE * j, TILE * (j + 1))
            hi = slice(HALF // 2 + TILE * j, HALF // 2 + TILE * (j + 1))
            far_ref[:, lo] = (far_in[:, lo].astype(F32) + a[rows].astype(F32)).astype(BF)
            near_ref[:, hi] = (near_in[:, hi].astype(F32) + b[rows].astype(F32)).astype(BF)

    return pl.pallas_call(
        kernel,
        out_shape=[jax.ShapeDtypeStruct((COLS, HALF), BF)] * 2,
        in_specs=[VMEM] * 4,
        out_specs=[VMEM] * 2,
        input_output_aliases={0: 0, 1: 1},
        compiler_params=pltpu.CompilerParams(vmem_limit_bytes=SMALL_CAP),
        cost_estimate=pl.CostEstimate(flops=COLS * HALF, bytes_accessed=3 << 20, transcendentals=0),
        name="add_beyond",
    )(near, far, from_near, from_far)


CORR_ONE = 1.0 - 0.8**20
CORR_TWO = 1.0 - 0.99**20


def accrue(g, m1, m2, e, w):
    top = (0.4 / CORR_ONE) * m1.astype(F32) + (0.1 / CORR_ONE) * g
    v = (0.99 / CORR_TWO) * m2.astype(F32) + (0.01 / CORR_TWO) * (g * g)
    low = v * lax.rsqrt(v) + 1e-08
    near = pltpu.reciprocal(low, approx=True)
    delta = top * (near * (2.0 - low * near)) + 0.05 * w
    return (0.95 * e.astype(F32) + delta).astype(BF)


def total(refs):
    return refs[0][...] + functools.reduce(jnp.add, [r[...].astype(F32) for r in refs[1:]])


def sent_tiles(ids, sels, m1, m2, err, weights):
    def kernel(ids_ref, *refs):
        a, b = refs[0:4], refs[4:8]
        m1_ref, m2_ref, e_ref, w_ref, out, grad = refs[8:]
        put_ids(out, SLOTS * COLS, lambda s: ids_ref[s])
        for k in range(SLOTS):
            t = ids_ref[k]
            rows = slice(COLS * k, COLS * (k + 1))

            @pl.when(t < 0)
            def _():
                out[rows] = jnp.zeros((COLS, TILE), BF)

            @pl.when(t >= 0)
            def _():
                @pl.when(t < HALF // TILE)
                def _():
                    grad[...] = total([r.at[rows] for r in a])

                @pl.when(t >= HALF // TILE)
                def _():
                    grad[...] = total([r.at[rows] for r in b])

                at = pl.ds(pl.multiple_of(t * TILE, TILE), TILE)
                out[rows] = accrue(grad[...], m1_ref[:, at], m2_ref[:, at], e_ref[:, at], w_ref[:, at])

    return pl.pallas_call(
        kernel,
        out_shape=jax.ShapeDtypeStruct((PIECE, TILE), BF),
        in_specs=[pl.BlockSpec(memory_space=pltpu.SMEM)] + [VMEM] * 12,
        out_specs=VMEM,
        scratch_shapes=[pltpu.VMEM((COLS, TILE), F32)],
        compiler_params=pltpu.CompilerParams(vmem_limit_bytes=SMALL_CAP),
        cost_estimate=pl.CostEstimate(flops=20 * SLOTS * COLS * TILE, bytes_accessed=2 << 20, transcendentals=0),
        name="sent_tiles",
    )(ids, *sels, m1, m2, err, weights)


def tied(vs, after):
    n = len(vs)
    return pl.pallas_call(
        lambda *refs: None,
        out_shape=[jax.ShapeDtypeStruct(v.shape, v.dtype) for v in vs],
        in_specs=[pl.BlockSpec(memory_space=pl.ANY)] * (n + len(after)),
        out_specs=[pl.BlockSpec(memory_space=pl.ANY)] * n,
        input_output_aliases={i: i for i in range(n)},
        compiler_params=pltpu.CompilerParams(vmem_limit_bytes=SMALL_CAP),
        cost_estimate=pl.CostEstimate(flops=0, bytes_accessed=0, transcendentals=0),
        name="tied",
    )(*vs, *after)


def pair(mine, other, *after):
    def kernel(a, b, *rest):
        rest[-1][0:PIECE] = a[...]
        rest[-1][PIECE:] = b[...]

    return pl.pallas_call(
        kernel,
        out_shape=jax.ShapeDtypeStruct((2 * PIECE, TILE), BF),
        in_specs=[VMEM] * 2 + [pl.BlockSpec(memory_space=pl.ANY)] * len(after),
        out_specs=VMEM,
        compiler_params=pltpu.CompilerParams(vmem_limit_bytes=SMALL_CAP),
        cost_estimate=pl.CostEstimate(flops=0, bytes_accessed=8 * PIECE * TILE, transcendentals=0),
        name="pair",
    )(mine, other, *after)


def own_half(both, *after):
    def kernel(ref, *rest):
        rest[-1][...] = ref[0:PIECE]

    return pl.pallas_call(
        kernel,
        out_shape=jax.ShapeDtypeStruct((PIECE, TILE), BF),
        in_specs=[VMEM] + [pl.BlockSpec(memory_space=pl.ANY)] * len(after),
        out_specs=VMEM,
        compiler_params=pltpu.CompilerParams(vmem_limit_bytes=SMALL_CAP),
        cost_estimate=pl.CostEstimate(flops=0, bytes_accessed=4 * PIECE * TILE, transcendentals=0),
        name="own_half",
    )(both, *after)


def keep_error(ids, grads, m1, m2, err, weights, part, before=None):
    width = 512
    tiles = width // TILE
    steps = HALF // width

    def kernel(ids_ref, g0, g1, g2, m1_ref, m2_ref, e_ref, w_ref, *rest):
        out, flag, kept, sems = rest[-4:]
        flag[...] = jnp.zeros_like(flag)
        copies = []
        for i in range(steps):
            for j in range(tiles):
                at = slice(width * i + TILE * j, width * i + TILE * (j + 1))
                to = slice(part * HALF + at.start, part * HALF + at.stop)
                g = total([r.at[:, at] for r in (g0, g1, g2)])
                kept[:, at] = accrue(g, m1_ref[:, to], m2_ref[:, to], e_ref[:, to], w_ref[:, to])
            for k in range(SLOTS):
                j = ids_ref[k] - part * (HALF // TILE) - i * tiles

                @pl.when((j >= 0) & (j < tiles))
                def _():
                    kept[:, pl.ds(pl.multiple_of(width * i + j * TILE, TILE), TILE)] = jnp.zeros((COLS, TILE), BF)

            copies.append(
                pltpu.make_async_copy(
                    kept.at[:, pl.ds(width * i, width)],
                    out.at[:, pl.ds(part * HALF + width * i, width)],
                    sems.at[i],
                )
            )
            copies[-1].start()
        for c in copies:
            c.wait()

    hbm = pl.BlockSpec(memory_space=pltpu.HBM)
    more = [] if before is None else [before]
    return pl.pallas_call(
        kernel,
        out_shape=[jax.ShapeDtypeStruct((COLS, FEATS), BF), jax.ShapeDtypeStruct((8, TILE), F32)],
        in_specs=[pl.BlockSpec(memory_space=pltpu.SMEM)] + [VMEM] * 7 + [hbm] * len(more),
        out_specs=[hbm, VMEM],
        input_output_aliases={8: 0} if more else {},
        scratch_shapes=[pltpu.VMEM((COLS, HALF), BF), pltpu.SemaphoreType.DMA((steps,))],
        compiler_params=pltpu.CompilerParams(vmem_limit_bytes=SMALL_CAP),
        cost_estimate=pl.CostEstimate(flops=20 * COLS * HALF, bytes_accessed=5 << 20, transcendentals=0),
        name="keep_error",
    )(ids, *grads, m1, m2, err, weights, *more)


def add_tiles(pieces, after):
    n = len(pieces)
    halves = sum(p.shape[0] // PIECE for p in pieces)

    def kernel(*refs):
        ins, (out, acc, listed) = refs[:n], refs[-3:]
        where = [(ref, h * PIECE) for ref in ins for h in range(ref.shape[0] // PIECE)]
        for at, (ref, row) in enumerate(where):
            for k, t in enumerate(get_ids(ref[row + SLOTS * COLS : row + PIECE])):
                listed[SLOTS * at + k] = t
        acc[...] = jnp.zeros_like(acc)
        for at, (ref, row) in enumerate(where):
            for k in range(SLOTS):
                t = listed[SLOTS * at + k]

                @pl.when(t >= 0)
                def _():
                    lanes = pl.ds(pl.multiple_of(t * TILE, TILE), TILE)
                    begin = row + COLS * k
                    acc[:, lanes] = acc[:, lanes] + ref[begin : begin + COLS].astype(F32)

        out[...] = (acc[...] * (1.0 / 16.0)).astype(BF)

    return pl.pallas_call(
        kernel,
        out_shape=jax.ShapeDtypeStruct((COLS, FEATS), BF),
        in_specs=[VMEM] * n + [pl.BlockSpec(memory_space=pl.ANY)] * len(after),
        scratch_shapes=[pltpu.VMEM((COLS, FEATS), F32), pltpu.SMEM((halves * SLOTS,), jnp.int32)],
        compiler_params=pltpu.CompilerParams(vmem_limit_bytes=SMALL_CAP),
        cost_estimate=pl.CostEstimate(flops=64 * 64 * 128, bytes_accessed=3 << 20, transcendentals=0),
        name="add_tiles",
    )(*pieces, *after)


def outer(mine, other, weights, momentum):
    width = 512
    steps = FEATS // width

    def kernel(m_ref, o_ref, w_ref, v_ref, w_out, v_out, w_new, v_new, sems):
        copies = []
        for i in range(steps):
            at = slice(width * i, width * (i + 1))
            agg = m_ref[:, at].astype(F32) + o_ref[:, at].astype(F32)
            vel = 0.9 * v_ref[:, at].astype(F32) + agg
            w_new[:, at] = w_ref[:, at] - 0.7 * (agg + 0.9 * vel)
            v_new[:, at] = vel.astype(BF)
            lanes = pl.ds(width * i, width)
            copies.append(pltpu.make_async_copy(w_new.at[:, lanes], w_out.at[:, lanes], sems.at[0, i]))
            copies.append(pltpu.make_async_copy(v_new.at[:, lanes], v_out.at[:, lanes], sems.at[1, i]))
            copies[-2].start()
            copies[-1].start()
        for c in copies:
            c.wait()

    hbm = pl.BlockSpec(memory_space=pltpu.HBM)
    return pl.pallas_call(
        kernel,
        out_shape=[jax.ShapeDtypeStruct((COLS, FEATS), F32), jax.ShapeDtypeStruct((COLS, FEATS), BF)],
        in_specs=[VMEM] * 4,
        out_specs=[hbm, hbm],
        scratch_shapes=[pltpu.VMEM((COLS, FEATS), F32), pltpu.VMEM((COLS, FEATS), BF), pltpu.SemaphoreType.DMA((2, steps))],
        compiler_params=pltpu.CompilerParams(vmem_limit_bytes=SMALL_CAP),
        cost_estimate=pl.CostEstimate(flops=6 * COLS * FEATS, bytes_accessed=8 << 20, transcendentals=0),
        name="outer",
    )(mine, other, weights, momentum)


def per_device(tokens, out_grad, weights, moment_one, moment_two, error_buf, momentum, tile_lists):
    tp = lax.axis_index("tp")
    ids = tile_lists[0, 0]
    place = jnp.concatenate([jnp.stack([tp // N, lax.rem(tp, N)]).astype(jnp.int32), ids])
    pos = place[:2]
    tok = tokens[0]
    og4 = out_grad[0].reshape(N, N, ROWS, COLS)
    state = (moment_one[0], moment_two[0], error_buf[0], weights)

    m = pack(place, tok, og4)
    yp, ym, xp, xm = along_y(m[0], 1), along_y(m[1], 3), along_x(m[2], 1), along_x(m[3], 3)
    y1, y2 = along_y(relay(yp, 1), 1), along_y(relay(ym, 3), 3)
    x1, x2 = along_x(relay(xp, 1), 1), along_x(relay(xm, 3), 3)

    ra = gather(pos, ids, og4, xp, xm, tok, yp, ym, 0)
    rb = gather(pos, ids, og4, yp, ym, tok, xp, xm, 1)
    pa = partials(pos, ra, x1, x2, y1, y2, 0, rb[1])
    sa = [pa[3], along_x(pa[5], 1), along_x(pa[4], 3), along_x(pa[6], 2)]
    pb = partials(pos, rb, y1, y2, x1, x2, 1, pa[3])
    (op_b,) = tied([pb[6]], sa[1:2])
    sb = [pb[3], along_y(pb[5], 1), along_y(pb[4], 3), along_y(op_b, 2)]
    near_a, far_a = add_beyond(pa[1], pa[2], sa[1], sa[2])
    near_b, far_b = add_beyond(pb[1], pb[2], sb[1], sb[2])
    ga = [pa[0], along_x(far_a, 1), along_x(near_a, 3)]
    gb = [pb[0], along_y(far_b, 1), along_y(near_b, 3)]

    mine = sent_tiles(ids, sa + sb, *state)
    own = pair(mine, across(mine))
    z1, z2 = onward(own, 1), onward(own, 2)
    z3, z4 = onward(z2, 1), onward(own_half(z2), 2)
    error_new, flag = keep_error(ids, ga, *state, 0)
    error_new, flag = keep_error(ids, gb, *state, 1, error_new)
    agg = add_tiles([mine, z1, z2, z3, z4], [flag])
    weights_new, momentum_new = outer(agg, across(agg), weights, momentum)

    return (weights_new, error_new[None], momentum_new)


def solution(mesh):
    return jax.shard_map(
        per_device,
        mesh=mesh,
        in_specs=(
            P("rep", "tp", None),
            P("rep", None, "tp"),
            P("tp", None),
            P("rep", "tp", None),
            P("rep", "tp", None),
            P("rep", "tp", None),
            P("tp", None),
            P("rep", "tp", None),
        ),
        out_specs=(P("tp", None), P("rep", "tp", None), P("tp", None)),
        check_vma=False,
    )
```

```python
import functools

import jax
import jax.numpy as jnp
from jax import lax
from jax.experimental import pallas as pl
from jax.experimental.pallas import tpu as pltpu
from jax.sharding import PartitionSpec as P

N = 4
ROWS = 192
HALF = 2048
COLS = 128
TILE = 128
FEATS = 4096
SLOTS = 4
PIECE = SLOTS * COLS + 16
T_ROWS = HALF // TILE * ROWS
O_ROWS = N * ROWS
IDS = 16
FIRST = T_ROWS + O_ROWS + O_ROWS // 2 + IDS
RELAY = T_ROWS // 2 + O_ROWS // 2 + IDS
BF = jnp.bfloat16
F32 = jnp.float32
SMALL_CAP = 8 * 1024 * 1024
PACK_CAP = 48 * 1024 * 1024
VMEM = pl.BlockSpec(memory_space=pltpu.VMEM)


def along_x(v, s):
    return lax.ppermute(v, "tp", [(N * a + b, N * ((a + s) % N) + b) for a in range(N) for b in range(N)])


def along_y(v, s):
    return lax.ppermute(v, "tp", [(N * a + b, N * a + (b + s) % N) for a in range(N) for b in range(N)])


def onward(v, s):
    pairs = [(2 * a, 2 * ((a + s) % 8)) for a in range(8)] + [(2 * a + 1, 2 * ((a + 8 - s) % 8) + 1) for a in range(8)]
    return lax.ppermute(v, "rep", pairs)


def across(v):
    return lax.ppermute(v, "rep", [(2 * a + c, 2 * a + 1 - c) for a in range(8) for c in range(2)])


def put_ids(ref, row, read):
    at = lax.broadcasted_iota(jnp.int32, (IDS, TILE), 0)
    v = jnp.zeros((IDS, TILE), jnp.int32)
    for k in range(SLOTS):
        v = jnp.where(at == k, read(k) + 1, v)
    ref[row : row + IDS] = v.astype(F32).astype(BF)


def get_ids(block):
    at = lax.broadcasted_iota(jnp.int32, (IDS, TILE), 0)
    lane = lax.broadcasted_iota(jnp.int32, (IDS, TILE), 1)
    scale = jnp.where(at == 0, 1.0, jnp.where(at == 1, 64.0, jnp.where(at == 2, 4096.0, 262144.0)))
    scale = jnp.where((lane == 0) & (at < SLOTS), scale, 0.0)
    code = jnp.sum(block.astype(F32) * scale).astype(jnp.int32)
    return [((code >> (6 * k)) & 63) - 1 for k in range(SLOTS)]


def pack(place, tokens, og4):
    routes = [(0, 1), (0, 3), (1, 1), (1, 3)]

    def kernel(place_ref, tok_hbm, og, *rest):
        outs, (tok, sems) = rest[:4], rest[4:]
        copies = []
        for c in range(4):
            lanes = pl.ds(HALF // 2 * c, HALF // 2)
            copies.append(pltpu.make_async_copy(tok_hbm.at[:, lanes], tok.at[:, lanes], sems.at[c]))
            copies[-1].start()
        for out, (part, shift) in zip(outs, routes, strict=True):
            here = place_ref[1 - part]
            near, far = lax.rem(here + shift, N), lax.rem(here + 2, N)
            lo = 0 if shift == 1 else 2
            for i in range(N + 2):
                k, other = (i, near) if i < N else (lo + i - N, far)
                row = T_ROWS + ROWS * i
                out[row : row + ROWS] = og[k, other] if part == 0 else og[other, k]
            put_ids(out, FIRST - IDS, lambda k: place_ref[2 + k])
        tiles = HALF // TILE
        for c in range(4):
            copies[c].wait()
            for out in outs[2 * (c // 2) : 2 * (c // 2) + 2]:
                for j in range(tiles // 2 * (c % 2), tiles // 2 * (c % 2 + 1)):
                    at = HALF * (c // 2) + TILE * j
                    out[ROWS * j : ROWS * (j + 1)] = tok[:, at : at + TILE]

    return pl.pallas_call(
        kernel,
        out_shape=[jax.ShapeDtypeStruct((FIRST, TILE), BF)] * 4,
        in_specs=[pl.BlockSpec(memory_space=pltpu.SMEM), pl.BlockSpec(memory_space=pltpu.HBM), VMEM],
        out_specs=[VMEM] * 4,
        scratch_shapes=[pltpu.VMEM((ROWS, FEATS), BF), pltpu.SemaphoreType.DMA((4,))],
        cost_estimate=pl.CostEstimate(flops=0, bytes_accessed=16 * FIRST * TILE, transcendentals=0),
        compiler_params=pltpu.CompilerParams(vmem_limit_bytes=PACK_CAP),
        name="pack",
    )(place, tokens, og4)


def relay(message, shift):
    lo = 0 if shift == 1 else ROWS // 2
    hi = lo + ROWS // 2

    def kernel(ref, out):
        for j in range(HALF // TILE):
            out[ROWS // 2 * j : ROWS // 2 * (j + 1)] = ref[ROWS * j + lo : ROWS * j + hi]
        out[T_ROWS // 2 :] = ref[T_ROWS + O_ROWS :]

    return pl.pallas_call(
        kernel,
        out_shape=jax.ShapeDtypeStruct((RELAY, TILE), BF),
        in_specs=[VMEM],
        out_specs=VMEM,
        compiler_params=pltpu.CompilerParams(vmem_limit_bytes=SMALL_CAP),
        cost_estimate=pl.CostEstimate(flops=0, bytes_accessed=4 * RELAY * TILE, transcendentals=0),
        name="relay",
    )(message)


def gather(pos, ids, og4, near_o, far_o, tokens, near_t, far_t, part):
    def kernel(pos_ref, ids_ref, own_o, n_o, f_o, t, l, r, rhs, turned, listed, lhs):
        x, y = pos_ref[0], pos_ref[1]
        here = pos_ref[1 - part]
        for s, d in enumerate((0, N - 1, 1, 2)):
            k = lax.rem(here + d, N)
            rows = slice(ROWS * s, ROWS * (s + 1))
            their = pl.ds(pl.multiple_of(T_ROWS + k * ROWS, ROWS), ROWS)
            lhs[rows, 0:COLS] = own_o[x, k] if part == 0 else own_o[k, y]
            lhs[rows, COLS : 2 * COLS] = n_o[their]
            lhs[rows, 2 * COLS : 3 * COLS] = f_o[their]
        for p in range(3):
            at = slice(COLS * p, COLS * (p + 1))
            turned[at] = lhs[:, at].T
        for p, ref in enumerate((None, n_o, f_o)):
            found = [ids_ref[k] for k in range(SLOTS)] if ref is None else get_ids(ref[FIRST - IDS :])
            for k in range(SLOTS):
                listed[SLOTS * p + k] = found[k] - part * (HALF // TILE)
        rhs[0:ROWS] = t[:, HALF * part : HALF * (part + 1)]
        for j in range(HALF // TILE):
            at = slice(TILE * j, TILE * (j + 1))
            rows = slice(ROWS * j, ROWS * (j + 1))
            rhs[ROWS : 2 * ROWS, at] = l[rows]
            rhs[2 * ROWS : 3 * ROWS, at] = r[rows]

    smem = pl.BlockSpec(memory_space=pltpu.SMEM)
    return pl.pallas_call(
        kernel,
        out_shape=[
            jax.ShapeDtypeStruct((N * ROWS, HALF), BF),
            jax.ShapeDtypeStruct((N * COLS, N * ROWS), BF),
            jax.ShapeDtypeStruct((N * SLOTS,), jnp.int32),
        ],
        in_specs=[smem, smem] + [VMEM] * 6,
        out_specs=[VMEM, VMEM, smem],
        scratch_shapes=[pltpu.VMEM((N * ROWS, 3 * COLS), BF)],
        compiler_params=pltpu.CompilerParams(vmem_limit_bytes=SMALL_CAP),
        cost_estimate=pl.CostEstimate(flops=0, bytes_accessed=8 << 20, transcendentals=0),
        name="gather",
    )(pos, ids, og4, near_o, far_o, tokens, near_t, far_t)


def partials(pos, ready, lo_o, hi_o, op1, op2, part, *after):
    width = 512
    half = ROWS // 2
    tiles = HALF // TILE

    def kernel(pos_ref, listed, lo, hi, a, b, rhs_in, turned_in, *rest):
        own, near, far, own_sel, to_near, to_far, op_sel, rhs, turned, lhs, op, beyond, found = rest[len(after) :]
        op[0 : O_ROWS // 2] = lo[T_ROWS // 2 : T_ROWS // 2 + O_ROWS // 2]
        op[O_ROWS // 2 :] = hi[T_ROWS // 2 : T_ROWS // 2 + O_ROWS // 2]
        here = pos_ref[1 - part]
        for s, d in enumerate((0, N - 1, 1, 2)):
            k = lax.rem(here + d, N)
            lhs[ROWS * s : ROWS * (s + 1)] = op[pl.ds(pl.multiple_of(k * ROWS, ROWS), ROWS)]
        turned[3 * COLS :] = lhs[...].T
        for k in range(3 * SLOTS):
            found[k] = listed[k]
        for k, t in enumerate(get_ids(lo[RELAY - IDS :])):
            found[3 * SLOTS + k] = t - part * tiles
        for j in range(tiles):
            at = slice(TILE * j, TILE * (j + 1))
            rhs[3 * ROWS : 3 * ROWS + half, at] = a[half * j : half * (j + 1)]
            rhs[3 * ROWS + half :, at] = b[half * j : half * (j + 1)]
        for i in range(HALF // width):
            at = slice(width * i, width * (i + 1))
            res = jnp.dot(turned[...], rhs[:, at], preferred_element_type=F32)
            own[:, at] = res[0:COLS]
            near[:, at] = res[COLS : 2 * COLS].astype(BF)
            far[:, at] = res[2 * COLS : 3 * COLS].astype(BF)
            beyond[:, at] = res[3 * COLS :].astype(BF)
        for j in range(tiles):
            out = to_far if j < tiles // 2 else to_near
            row = SLOTS * COLS + COLS * (j % (tiles // 2))
            out[row : row + COLS] = beyond[:, TILE * j : TILE * (j + 1)]
        for p, (out, sel) in enumerate(((own, own_sel), (near, to_near), (far, to_far), (beyond, op_sel))):
            for k in range(SLOTS):
                t = found[SLOTS * p + k]

                @pl.when((t >= 0) & (t < tiles))
                def _():
                    sel[COLS * k : COLS * (k + 1)] = out[:, pl.ds(pl.multiple_of(t * TILE, TILE), TILE)]

    smem = pl.BlockSpec(memory_space=pltpu.SMEM)
    rhs, turned, listed = ready
    shape = jax.ShapeDtypeStruct
    wide, message, few = (COLS, HALF), (SLOTS * COLS + COLS * tiles // 2, TILE), (SLOTS * COLS, TILE)
    return pl.pallas_call(
        kernel,
        out_shape=[shape(wide, F32), shape(wide, BF), shape(wide, BF), shape(few, F32), shape(message, BF), shape(message, BF), shape(few, BF)]
        + [shape(v.shape, v.dtype) for v in (rhs, turned)],
        in_specs=[smem, smem] + [VMEM] * 6 + [pl.BlockSpec(memory_space=pl.ANY)] * len(after),
        out_specs=[VMEM] * 9,
        input_output_aliases={6: 7, 7: 8},
        scratch_shapes=[
            pltpu.VMEM((N * ROWS, COLS), BF),
            pltpu.VMEM((O_ROWS, TILE), BF),
            pltpu.VMEM(wide, BF),
            pltpu.SMEM((N * SLOTS,), jnp.int32),
        ],
        compiler_params=pltpu.CompilerParams(vmem_limit_bytes=SMALL_CAP),
        cost_estimate=pl.CostEstimate(flops=2 * 768 * 512 * HALF, bytes_accessed=8 << 20, transcendentals=0),
        name="partials",
    )(pos, listed, lo_o, hi_o, op1, op2, rhs, turned, *after)


def add_beyond(near, far, from_near, from_far):
    tiles = HALF // TILE // 2

    def kernel(near_in, far_in, a, b, near_ref, far_ref):
        for j in range(tiles):
            rows = slice(SLOTS * COLS + COLS * j, SLOTS * COLS + COLS * (j + 1))
            lo = slice(TILE * j, TILE * (j + 1))
            hi = slice(HALF // 2 + TILE * j, HALF // 2 + TILE * (j + 1))
            far_ref[:, lo] = (far_in[:, lo].astype(F32) + a[rows].astype(F32)).astype(BF)
            near_ref[:, hi] = (near_in[:, hi].astype(F32) + b[rows].astype(F32)).astype(BF)

    return pl.pallas_call(
        kernel,
        out_shape=[jax.ShapeDtypeStruct((COLS, HALF), BF)] * 2,
        in_specs=[VMEM] * 4,
        out_specs=[VMEM] * 2,
        input_output_aliases={0: 0, 1: 1},
        compiler_params=pltpu.CompilerParams(vmem_limit_bytes=SMALL_CAP),
        cost_estimate=pl.CostEstimate(flops=COLS * HALF, bytes_accessed=3 << 20, transcendentals=0),
        name="add_beyond",
    )(near, far, from_near, from_far)


CORR_ONE = 1.0 - 0.8**20
CORR_TWO = 1.0 - 0.99**20


def accrue(g, m1, m2, e, w):
    top = (0.4 / CORR_ONE) * m1.astype(F32) + (0.1 / CORR_ONE) * g
    v = (0.99 / CORR_TWO) * m2.astype(F32) + (0.01 / CORR_TWO) * (g * g)
    low = v * lax.rsqrt(v) + 1e-08
    near = pltpu.reciprocal(low, approx=True)
    delta = top * (near * (2.0 - low * near)) + 0.05 * w
    return (0.95 * e.astype(F32) + delta).astype(BF)


def total(refs):
    return refs[0][...] + functools.reduce(jnp.add, [r[...].astype(F32) for r in refs[1:]])


def sent_tiles(ids, sels, m1, m2, err, weights):
    def kernel(ids_ref, *refs):
        a, b = refs[0:4], refs[4:8]
        m1_ref, m2_ref, e_ref, w_ref, out, grad = refs[8:]
        put_ids(out, SLOTS * COLS, lambda s: ids_ref[s])
        for k in range(SLOTS):
            t = ids_ref[k]
            rows = slice(COLS * k, COLS * (k + 1))

            @pl.when(t < 0)
            def _():
                out[rows] = jnp.zeros((COLS, TILE), BF)

            @pl.when(t >= 0)
            def _():
                @pl.when(t < HALF // TILE)
                def _():
                    grad[...] = total([r.at[rows] for r in a])

                @pl.when(t >= HALF // TILE)
                def _():
                    grad[...] = total([r.at[rows] for r in b])

                at = pl.ds(pl.multiple_of(t * TILE, TILE), TILE)
                out[rows] = accrue(grad[...], m1_ref[:, at], m2_ref[:, at], e_ref[:, at], w_ref[:, at])

    return pl.pallas_call(
        kernel,
        out_shape=jax.ShapeDtypeStruct((PIECE, TILE), BF),
        in_specs=[pl.BlockSpec(memory_space=pltpu.SMEM)] + [VMEM] * 12,
        out_specs=VMEM,
        scratch_shapes=[pltpu.VMEM((COLS, TILE), F32)],
        compiler_params=pltpu.CompilerParams(vmem_limit_bytes=SMALL_CAP),
        cost_estimate=pl.CostEstimate(flops=20 * SLOTS * COLS * TILE, bytes_accessed=2 << 20, transcendentals=0),
        name="sent_tiles",
    )(ids, *sels, m1, m2, err, weights)


def tied(vs, after):
    n = len(vs)
    return pl.pallas_call(
        lambda *refs: None,
        out_shape=[jax.ShapeDtypeStruct(v.shape, v.dtype) for v in vs],
        in_specs=[pl.BlockSpec(memory_space=pl.ANY)] * (n + len(after)),
        out_specs=[pl.BlockSpec(memory_space=pl.ANY)] * n,
        input_output_aliases={i: i for i in range(n)},
        compiler_params=pltpu.CompilerParams(vmem_limit_bytes=SMALL_CAP),
        cost_estimate=pl.CostEstimate(flops=0, bytes_accessed=0, transcendentals=0),
        name="tied",
    )(*vs, *after)


def pair(mine, other, *after):
    def kernel(a, b, *rest):
        rest[-1][0:PIECE] = a[...]
        rest[-1][PIECE:] = b[...]

    return pl.pallas_call(
        kernel,
        out_shape=jax.ShapeDtypeStruct((2 * PIECE, TILE), BF),
        in_specs=[VMEM] * 2 + [pl.BlockSpec(memory_space=pl.ANY)] * len(after),
        out_specs=VMEM,
        compiler_params=pltpu.CompilerParams(vmem_limit_bytes=SMALL_CAP),
        cost_estimate=pl.CostEstimate(flops=0, bytes_accessed=8 * PIECE * TILE, transcendentals=0),
        name="pair",
    )(mine, other, *after)


def own_half(both, *after):
    def kernel(ref, *rest):
        rest[-1][...] = ref[0:PIECE]

    return pl.pallas_call(
        kernel,
        out_shape=jax.ShapeDtypeStruct((PIECE, TILE), BF),
        in_specs=[VMEM] + [pl.BlockSpec(memory_space=pl.ANY)] * len(after),
        out_specs=VMEM,
        compiler_params=pltpu.CompilerParams(vmem_limit_bytes=SMALL_CAP),
        cost_estimate=pl.CostEstimate(flops=0, bytes_accessed=4 * PIECE * TILE, transcendentals=0),
        name="own_half",
    )(both, *after)


def keep_error(ids, grads, m1, m2, err, weights, part, before=None):
    width = 512
    tiles = width // TILE
    steps = HALF // width

    def kernel(ids_ref, g0, g1, g2, m1_ref, m2_ref, e_ref, w_ref, *rest):
        out, flag, kept, sems = rest[-4:]
        flag[...] = jnp.zeros_like(flag)
        copies = []
        for i in range(steps):
            for j in range(tiles):
                at = slice(width * i + TILE * j, width * i + TILE * (j + 1))
                to = slice(part * HALF + at.start, part * HALF + at.stop)
                g = total([r.at[:, at] for r in (g0, g1, g2)])
                kept[:, at] = accrue(g, m1_ref[:, to], m2_ref[:, to], e_ref[:, to], w_ref[:, to])
            for k in range(SLOTS):
                j = ids_ref[k] - part * (HALF // TILE) - i * tiles

                @pl.when((j >= 0) & (j < tiles))
                def _():
                    kept[:, pl.ds(pl.multiple_of(width * i + j * TILE, TILE), TILE)] = jnp.zeros((COLS, TILE), BF)

            copies.append(
                pltpu.make_async_copy(
                    kept.at[:, pl.ds(width * i, width)],
                    out.at[:, pl.ds(part * HALF + width * i, width)],
                    sems.at[i],
                )
            )
            copies[-1].start()
        for c in copies:
            c.wait()

    hbm = pl.BlockSpec(memory_space=pltpu.HBM)
    more = [] if before is None else [before]
    return pl.pallas_call(
        kernel,
        out_shape=[jax.ShapeDtypeStruct((COLS, FEATS), BF), jax.ShapeDtypeStruct((8, TILE), F32)],
        in_specs=[pl.BlockSpec(memory_space=pltpu.SMEM)] + [VMEM] * 7 + [hbm] * len(more),
        out_specs=[hbm, VMEM],
        input_output_aliases={8: 0} if more else {},
        scratch_shapes=[pltpu.VMEM((COLS, HALF), BF), pltpu.SemaphoreType.DMA((steps,))],
        compiler_params=pltpu.CompilerParams(vmem_limit_bytes=SMALL_CAP),
        cost_estimate=pl.CostEstimate(flops=20 * COLS * HALF, bytes_accessed=5 << 20, transcendentals=0),
        name="keep_error",
    )(ids, *grads, m1, m2, err, weights, *more)


def add_tiles(pieces, after):
    n = len(pieces)
    halves = sum(p.shape[0] // PIECE for p in pieces)

    def kernel(*refs):
        ins, (out, acc, listed) = refs[:n], refs[-3:]
        where = [(ref, h * PIECE) for ref in ins for h in range(ref.shape[0] // PIECE)]
        for at, (ref, row) in enumerate(where):
            for k, t in enumerate(get_ids(ref[row + SLOTS * COLS : row + PIECE])):
                listed[SLOTS * at + k] = t
        acc[...] = jnp.zeros_like(acc)
        for at, (ref, row) in enumerate(where):
            for k in range(SLOTS):
                t = listed[SLOTS * at + k]

                @pl.when(t >= 0)
                def _():
                    lanes = pl.ds(pl.multiple_of(t * TILE, TILE), TILE)
                    begin = row + COLS * k
                    acc[:, lanes] = acc[:, lanes] + ref[begin : begin + COLS].astype(F32)

        out[...] = (acc[...] * (1.0 / 16.0)).astype(BF)

    return pl.pallas_call(
        kernel,
        out_shape=jax.ShapeDtypeStruct((COLS, FEATS), BF),
        in_specs=[VMEM] * n + [pl.BlockSpec(memory_space=pl.ANY)] * len(after),
        scratch_shapes=[pltpu.VMEM((COLS, FEATS), F32), pltpu.SMEM((halves * SLOTS,), jnp.int32)],
        compiler_params=pltpu.CompilerParams(vmem_limit_bytes=SMALL_CAP),
        cost_estimate=pl.CostEstimate(flops=64 * 64 * 128, bytes_accessed=3 << 20, transcendentals=0),
        name="add_tiles",
    )(*pieces, *after)


def outer(mine, other, weights, momentum):
    width = 512
    steps = FEATS // width

    def kernel(m_ref, o_ref, w_ref, v_ref, w_out, v_out, w_new, v_new, sems):
        copies = []
        for i in range(steps):
            at = slice(width * i, width * (i + 1))
            agg = m_ref[:, at].astype(F32) + o_ref[:, at].astype(F32)
            vel = 0.9 * v_ref[:, at].astype(F32) + agg
            w_new[:, at] = w_ref[:, at] - 0.7 * (agg + 0.9 * vel)
            v_new[:, at] = vel.astype(BF)
            lanes = pl.ds(width * i, width)
            copies.append(pltpu.make_async_copy(w_new.at[:, lanes], w_out.at[:, lanes], sems.at[0, i]))
            copies.append(pltpu.make_async_copy(v_new.at[:, lanes], v_out.at[:, lanes], sems.at[1, i]))
            copies[-2].start()
            copies[-1].start()
        for c in copies:
            c.wait()

    hbm = pl.BlockSpec(memory_space=pltpu.HBM)
    return pl.pallas_call(
        kernel,
        out_shape=[jax.ShapeDtypeStruct((COLS, FEATS), F32), jax.ShapeDtypeStruct((COLS, FEATS), BF)],
        in_specs=[VMEM] * 4,
        out_specs=[hbm, hbm],
        scratch_shapes=[pltpu.VMEM((COLS, FEATS), F32), pltpu.VMEM((COLS, FEATS), BF), pltpu.SemaphoreType.DMA((2, steps))],
        compiler_params=pltpu.CompilerParams(vmem_limit_bytes=SMALL_CAP),
        cost_estimate=pl.CostEstimate(flops=6 * COLS * FEATS, bytes_accessed=8 << 20, transcendentals=0),
        name="outer",
    )(mine, other, weights, momentum)


def per_device(tokens, out_grad, weights, moment_one, moment_two, error_buf, momentum, tile_lists):
    tp = lax.axis_index("tp")
    ids = tile_lists[0, 0]
    place = jnp.concatenate([jnp.stack([tp // N, lax.rem(tp, N)]).astype(jnp.int32), ids])
    pos = place[:2]
    tok = tokens[0]
    og4 = out_grad[0].reshape(N, N, ROWS, COLS)
    state = (moment_one[0], moment_two[0], error_buf[0], weights)

    m = pack(place, tok, og4)
    yp, ym, xp, xm = along_y(m[0], 1), along_y(m[1], 3), along_x(m[2], 1), along_x(m[3], 3)
    y1, y2 = along_y(relay(yp, 1), 1), along_y(relay(ym, 3), 3)
    x1, x2 = along_x(relay(xp, 1), 1), along_x(relay(xm, 3), 3)

    ra = gather(pos, ids, og4, xp, xm, tok, yp, ym, 0)
    rb = gather(pos, ids, og4, yp, ym, tok, xp, xm, 1)
    pa = partials(pos, ra, x1, x2, y1, y2, 0, rb[1])
    sa = [pa[3], along_x(pa[5], 1), along_x(pa[4], 3), along_x(pa[6], 2)]
    pb = partials(pos, rb, y1, y2, x1, x2, 1, pa[3])
    (op_b,) = tied([pb[6]], sa[1:2])
    sb = [pb[3], along_y(pb[5], 1), along_y(pb[4], 3), along_y(op_b, 2)]
    near_a, far_a = add_beyond(pa[1], pa[2], sa[1], sa[2])
    near_b, far_b = add_beyond(pb[1], pb[2], sb[1], sb[2])
    ga = [pa[0], along_x(far_a, 1), along_x(near_a, 3)]
    gb = [pb[0], along_y(far_b, 1), along_y(near_b, 3)]

    mine = sent_tiles(ids, sa + sb, *state)
    own = pair(mine, across(mine))
    z1, z2 = onward(own, 1), onward(own, 2)
    z3, z4 = onward(z2, 1), onward(own_half(z2), 2)
    error_new, flag = keep_error(ids, ga, *state, 0)
    error_new, flag = keep_error(ids, gb, *state, 1, error_new)
    agg = add_tiles([mine, z1, z2, z3, z4], [flag])
    weights_new, momentum_new = outer(agg, across(agg), weights, momentum)

    return (weights_new, error_new[None], momentum_new)


def solution(mesh):
    return jax.shard_map(
        per_device,
        mesh=mesh,
        in_specs=(
            P("rep", "tp", None),
            P("rep", None, "tp"),
            P("tp", None),
            P("rep", "tp", None),
            P("rep", "tp", None),
            P("rep", "tp", None),
            P("tp", None),
            P("rep", "tp", None),
        ),
        out_specs=(P("tp", None), P("rep", "tp", None), P("tp", None)),
        check_vma=False,
    )
```

```python
import functools

import jax
import jax.numpy as jnp
from jax import lax
from jax.experimental import pallas as pl
from jax.experimental.pallas import tpu as pltpu
from jax.sharding import PartitionSpec as P

N = 4
ROWS = 192
HALF = 2048
COLS = 128
TILE = 128
FEATS = 4096
SLOTS = 4
PIECE = SLOTS * COLS + 16
T_ROWS = HALF // TILE * ROWS
O_ROWS = N * ROWS
IDS = 16
FIRST = T_ROWS + O_ROWS + O_ROWS // 2 + IDS
RELAY = T_ROWS // 2 + O_ROWS // 2 + IDS
BF = jnp.bfloat16
F32 = jnp.float32
SMALL_CAP = 8 * 1024 * 1024
PACK_CAP = 48 * 1024 * 1024
VMEM = pl.BlockSpec(memory_space=pltpu.VMEM)


def along_x(v, s):
    return lax.ppermute(v, "tp", [(N * a + b, N * ((a + s) % N) + b) for a in range(N) for b in range(N)])


def along_y(v, s):
    return lax.ppermute(v, "tp", [(N * a + b, N * a + (b + s) % N) for a in range(N) for b in range(N)])


def onward(v, s):
    pairs = [(2 * a, 2 * ((a + s) % 8)) for a in range(8)] + [(2 * a + 1, 2 * ((a + 8 - s) % 8) + 1) for a in range(8)]
    return lax.ppermute(v, "rep", pairs)


def across(v):
    return lax.ppermute(v, "rep", [(2 * a + c, 2 * a + 1 - c) for a in range(8) for c in range(2)])


def put_ids(ref, row, read):
    at = lax.broadcasted_iota(jnp.int32, (IDS, TILE), 0)
    v = jnp.zeros((IDS, TILE), jnp.int32)
    for k in range(SLOTS):
        v = jnp.where(at == k, read(k) + 1, v)
    ref[row : row + IDS] = v.astype(F32).astype(BF)


def get_ids(block):
    at = lax.broadcasted_iota(jnp.int32, (IDS, TILE), 0)
    lane = lax.broadcasted_iota(jnp.int32, (IDS, TILE), 1)
    scale = jnp.where(at == 0, 1.0, jnp.where(at == 1, 64.0, jnp.where(at == 2, 4096.0, 262144.0)))
    scale = jnp.where((lane == 0) & (at < SLOTS), scale, 0.0)
    code = jnp.sum(block.astype(F32) * scale).astype(jnp.int32)
    return [((code >> (6 * k)) & 63) - 1 for k in range(SLOTS)]


def pack(place, tokens, og4):
    routes = [(0, 1), (0, 3), (1, 1), (1, 3)]

    def kernel(place_ref, tok_hbm, og, *rest):
        outs, (tok, sems) = rest[:4], rest[4:]
        copies = []
        for c in range(4):
            lanes = pl.ds(HALF // 2 * c, HALF // 2)
            copies.append(pltpu.make_async_copy(tok_hbm.at[:, lanes], tok.at[:, lanes], sems.at[c]))
            copies[-1].start()
        for out, (part, shift) in zip(outs, routes, strict=True):
            here = place_ref[1 - part]
            near, far = lax.rem(here + shift, N), lax.rem(here + 2, N)
            lo = 0 if shift == 1 else 2
            for i in range(N + 2):
                k, other = (i, near) if i < N else (lo + i - N, far)
                row = T_ROWS + ROWS * i
                out[row : row + ROWS] = og[k, other] if part == 0 else og[other, k]
            put_ids(out, FIRST - IDS, lambda k: place_ref[2 + k])
        tiles = HALF // TILE
        for c in range(4):
            copies[c].wait()
            for out in outs[2 * (c // 2) : 2 * (c // 2) + 2]:
                for j in range(tiles // 2 * (c % 2), tiles // 2 * (c % 2 + 1)):
                    at = HALF * (c // 2) + TILE * j
                    out[ROWS * j : ROWS * (j + 1)] = tok[:, at : at + TILE]

    return pl.pallas_call(
        kernel,
        out_shape=[jax.ShapeDtypeStruct((FIRST, TILE), BF)] * 4,
        in_specs=[pl.BlockSpec(memory_space=pltpu.SMEM), pl.BlockSpec(memory_space=pltpu.HBM), VMEM],
        out_specs=[VMEM] * 4,
        scratch_shapes=[pltpu.VMEM((ROWS, FEATS), BF), pltpu.SemaphoreType.DMA((4,))],
        cost_estimate=pl.CostEstimate(flops=0, bytes_accessed=16 * FIRST * TILE, transcendentals=0),
        compiler_params=pltpu.CompilerParams(vmem_limit_bytes=PACK_CAP),
        name="pack",
    )(place, tokens, og4)


def relay(message, shift):
    lo = 0 if shift == 1 else ROWS // 2
    hi = lo + ROWS // 2

    def kernel(ref, out):
        for j in range(HALF // TILE):
            out[ROWS // 2 * j : ROWS // 2 * (j + 1)] = ref[ROWS * j + lo : ROWS * j + hi]
        out[T_ROWS // 2 :] = ref[T_ROWS + O_ROWS :]

    return pl.pallas_call(
        kernel,
        out_shape=jax.ShapeDtypeStruct((RELAY, TILE), BF),
        in_specs=[VMEM],
        out_specs=VMEM,
        compiler_params=pltpu.CompilerParams(vmem_limit_bytes=SMALL_CAP),
        cost_estimate=pl.CostEstimate(flops=0, bytes_accessed=4 * RELAY * TILE, transcendentals=0),
        name="relay",
    )(message)


def gather(pos, ids, og4, near_o, far_o, tokens, near_t, far_t, part):
    def kernel(pos_ref, ids_ref, own_o, n_o, f_o, t, l, r, rhs, turned, listed, lhs):
        x, y = pos_ref[0], pos_ref[1]
        here = pos_ref[1 - part]
        for s, d in enumerate((0, N - 1, 1, 2)):
            k = lax.rem(here + d, N)
            rows = slice(ROWS * s, ROWS * (s + 1))
            their = pl.ds(pl.multiple_of(T_ROWS + k * ROWS, ROWS), ROWS)
            lhs[rows, 0:COLS] = own_o[x, k] if part == 0 else own_o[k, y]
            lhs[rows, COLS : 2 * COLS] = n_o[their]
            lhs[rows, 2 * COLS : 3 * COLS] = f_o[their]
        for p in range(3):
            at = slice(COLS * p, COLS * (p + 1))
            turned[at] = lhs[:, at].T
        for p, ref in enumerate((None, n_o, f_o)):
            found = [ids_ref[k] for k in range(SLOTS)] if ref is None else get_ids(ref[FIRST - IDS :])
            for k in range(SLOTS):
                listed[SLOTS * p + k] = found[k] - part * (HALF // TILE)
        rhs[0:ROWS] = t[:, HALF * part : HALF * (part + 1)]
        for j in range(HALF // TILE):
            at = slice(TILE * j, TILE * (j + 1))
            rows = slice(ROWS * j, ROWS * (j + 1))
            rhs[ROWS : 2 * ROWS, at] = l[rows]
            rhs[2 * ROWS : 3 * ROWS, at] = r[rows]

    smem = pl.BlockSpec(memory_space=pltpu.SMEM)
    return pl.pallas_call(
        kernel,
        out_shape=[
            jax.ShapeDtypeStruct((N * ROWS, HALF), BF),
            jax.ShapeDtypeStruct((N * COLS, N * ROWS), BF),
            jax.ShapeDtypeStruct((N * SLOTS,), jnp.int32),
        ],
        in_specs=[smem, smem] + [VMEM] * 6,
        out_specs=[VMEM, VMEM, smem],
        scratch_shapes=[pltpu.VMEM((N * ROWS, 3 * COLS), BF)],
        compiler_params=pltpu.CompilerParams(vmem_limit_bytes=SMALL_CAP),
        cost_estimate=pl.CostEstimate(flops=0, bytes_accessed=8 << 20, transcendentals=0),
        name="gather",
    )(pos, ids, og4, near_o, far_o, tokens, near_t, far_t)


def partials(pos, ready, lo_o, hi_o, op1, op2, part, *after):
    width = 512
    half = ROWS // 2
    tiles = HALF // TILE

    def kernel(pos_ref, listed, lo, hi, a, b, rhs_in, turned_in, *rest):
        own, near, far, own_sel, to_near, to_far, op_sel, rhs, turned, lhs, op, beyond, found = rest[len(after) :]
        op[0 : O_ROWS // 2] = lo[T_ROWS // 2 : T_ROWS // 2 + O_ROWS // 2]
        op[O_ROWS // 2 :] = hi[T_ROWS // 2 : T_ROWS // 2 + O_ROWS // 2]
        here = pos_ref[1 - part]
        for s, d in enumerate((0, N - 1, 1, 2)):
            k = lax.rem(here + d, N)
            lhs[ROWS * s : ROWS * (s + 1)] = op[pl.ds(pl.multiple_of(k * ROWS, ROWS), ROWS)]
        turned[3 * COLS :] = lhs[...].T
        for k in range(3 * SLOTS):
            found[k] = listed[k]
        for k, t in enumerate(get_ids(lo[RELAY - IDS :])):
            found[3 * SLOTS + k] = t - part * tiles
        for j in range(tiles):
            at = slice(TILE * j, TILE * (j + 1))
            rhs[3 * ROWS : 3 * ROWS + half, at] = a[half * j : half * (j + 1)]
            rhs[3 * ROWS + half :, at] = b[half * j : half * (j + 1)]
        for i in range(HALF // width):
            at = slice(width * i, width * (i + 1))
            res = jnp.dot(turned[...], rhs[:, at], preferred_element_type=F32)
            own[:, at] = res[0:COLS]
            near[:, at] = res[COLS : 2 * COLS].astype(BF)
            far[:, at] = res[2 * COLS : 3 * COLS].astype(BF)
            beyond[:, at] = res[3 * COLS :].astype(BF)
        for j in range(tiles):
            out = to_far if j < tiles // 2 else to_near
            row = SLOTS * COLS + COLS * (j % (tiles // 2))
            out[row : row + COLS] = beyond[:, TILE * j : TILE * (j + 1)]
        for p, (out, sel) in enumerate(((own, own_sel), (near, to_near), (far, to_far), (beyond, op_sel))):
            for k in range(SLOTS):
                t = found[SLOTS * p + k]

                @pl.when((t >= 0) & (t < tiles))
                def _():
                    sel[COLS * k : COLS * (k + 1)] = out[:, pl.ds(pl.multiple_of(t * TILE, TILE), TILE)]

    smem = pl.BlockSpec(memory_space=pltpu.SMEM)
    rhs, turned, listed = ready
    shape = jax.ShapeDtypeStruct
    wide, message, few = (COLS, HALF), (SLOTS * COLS + COLS * tiles // 2, TILE), (SLOTS * COLS, TILE)
    return pl.pallas_call(
        kernel,
        out_shape=[shape(wide, F32), shape(wide, BF), shape(wide, BF), shape(few, F32), shape(message, BF), shape(message, BF), shape(few, BF)]
        + [shape(v.shape, v.dtype) for v in (rhs, turned)],
        in_specs=[smem, smem] + [VMEM] * 6 + [pl.BlockSpec(memory_space=pl.ANY)] * len(after),
        out_specs=[VMEM] * 9,
        input_output_aliases={6: 7, 7: 8},
        scratch_shapes=[
            pltpu.VMEM((N * ROWS, COLS), BF),
            pltpu.VMEM((O_ROWS, TILE), BF),
            pltpu.VMEM(wide, BF),
            pltpu.SMEM((N * SLOTS,), jnp.int32),
        ],
        compiler_params=pltpu.CompilerParams(vmem_limit_bytes=SMALL_CAP),
        cost_estimate=pl.CostEstimate(flops=2 * 768 * 512 * HALF, bytes_accessed=8 << 20, transcendentals=0),
        name="partials",
    )(pos, listed, lo_o, hi_o, op1, op2, rhs, turned, *after)


def add_beyond(near, far, from_near, from_far):
    tiles = HALF // TILE // 2

    def kernel(near_in, far_in, a, b, near_ref, far_ref):
        for j in range(tiles):
            rows = slice(SLOTS * COLS + COLS * j, SLOTS * COLS + COLS * (j + 1))
            lo = slice(TILE * j, TILE * (j + 1))
            hi = slice(HALF // 2 + TILE * j, HALF // 2 + TILE * (j + 1))
            far_ref[:, lo] = (far_in[:, lo].astype(F32) + a[rows].astype(F32)).astype(BF)
            near_ref[:, hi] = (near_in[:, hi].astype(F32) + b[rows].astype(F32)).astype(BF)

    return pl.pallas_call(
        kernel,
        out_shape=[jax.ShapeDtypeStruct((COLS, HALF), BF)] * 2,
        in_specs=[VMEM] * 4,
        out_specs=[VMEM] * 2,
        input_output_aliases={0: 0, 1: 1},
        compiler_params=pltpu.CompilerParams(vmem_limit_bytes=SMALL_CAP),
        cost_estimate=pl.CostEstimate(flops=COLS * HALF, bytes_accessed=3 << 20, transcendentals=0),
        name="add_beyond",
    )(near, far, from_near, from_far)


CORR_ONE = 1.0 - 0.8**20
CORR_TWO = 1.0 - 0.99**20


def accrue(g, m1, m2, e, w):
    top = (0.4 / CORR_ONE) * m1.astype(F32) + (0.1 / CORR_ONE) * g
    v = (0.99 / CORR_TWO) * m2.astype(F32) + (0.01 / CORR_TWO) * (g * g)
    low = v * lax.rsqrt(v) + 1e-08
    near = pltpu.reciprocal(low, approx=True)
    delta = top * (near * (2.0 - low * near)) + 0.05 * w
    return (0.95 * e.astype(F32) + delta).astype(BF)


def total(refs):
    return refs[0][...] + functools.reduce(jnp.add, [r[...].astype(F32) for r in refs[1:]])


def sent_tiles(ids, sels, m1, m2, err, weights):
    def kernel(ids_ref, *refs):
        a, b = refs[0:4], refs[4:8]
        m1_ref, m2_ref, e_ref, w_ref, out, grad = refs[8:]
        put_ids(out, SLOTS * COLS, lambda s: ids_ref[s])
        for k in range(SLOTS):
            t = ids_ref[k]
            rows = slice(COLS * k, COLS * (k + 1))

            @pl.when(t < 0)
            def _():
                out[rows] = jnp.zeros((COLS, TILE), BF)

            @pl.when(t >= 0)
            def _():
                @pl.when(t < HALF // TILE)
                def _():
                    grad[...] = total([r.at[rows] for r in a])

                @pl.when(t >= HALF // TILE)
                def _():
                    grad[...] = total([r.at[rows] for r in b])

                at = pl.ds(pl.multiple_of(t * TILE, TILE), TILE)
                out[rows] = accrue(grad[...], m1_ref[:, at], m2_ref[:, at], e_ref[:, at], w_ref[:, at])

    return pl.pallas_call(
        kernel,
        out_shape=jax.ShapeDtypeStruct((PIECE, TILE), BF),
        in_specs=[pl.BlockSpec(memory_space=pltpu.SMEM)] + [VMEM] * 12,
        out_specs=VMEM,
        scratch_shapes=[pltpu.VMEM((COLS, TILE), F32)],
        compiler_params=pltpu.CompilerParams(vmem_limit_bytes=SMALL_CAP),
        cost_estimate=pl.CostEstimate(flops=20 * SLOTS * COLS * TILE, bytes_accessed=2 << 20, transcendentals=0),
        name="sent_tiles",
    )(ids, *sels, m1, m2, err, weights)


def tied(vs, after):
    n = len(vs)
    return pl.pallas_call(
        lambda *refs: None,
        out_shape=[jax.ShapeDtypeStruct(v.shape, v.dtype) for v in vs],
        in_specs=[pl.BlockSpec(memory_space=pl.ANY)] * (n + len(after)),
        out_specs=[pl.BlockSpec(memory_space=pl.ANY)] * n,
        input_output_aliases={i: i for i in range(n)},
        compiler_params=pltpu.CompilerParams(vmem_limit_bytes=SMALL_CAP),
        cost_estimate=pl.CostEstimate(flops=0, bytes_accessed=0, transcendentals=0),
        name="tied",
    )(*vs, *after)


def pair(mine, other, *after):
    def kernel(a, b, *rest):
        rest[-1][0:PIECE] = a[...]
        rest[-1][PIECE:] = b[...]

    return pl.pallas_call(
        kernel,
        out_shape=jax.ShapeDtypeStruct((2 * PIECE, TILE), BF),
        in_specs=[VMEM] * 2 + [pl.BlockSpec(memory_space=pl.ANY)] * len(after),
        out_specs=VMEM,
        compiler_params=pltpu.CompilerParams(vmem_limit_bytes=SMALL_CAP),
        cost_estimate=pl.CostEstimate(flops=0, bytes_accessed=8 * PIECE * TILE, transcendentals=0),
        name="pair",
    )(mine, other, *after)


def own_half(both, *after):
    def kernel(ref, *rest):
        rest[-1][...] = ref[0:PIECE]

    return pl.pallas_call(
        kernel,
        out_shape=jax.ShapeDtypeStruct((PIECE, TILE), BF),
        in_specs=[VMEM] + [pl.BlockSpec(memory_space=pl.ANY)] * len(after),
        out_specs=VMEM,
        compiler_params=pltpu.CompilerParams(vmem_limit_bytes=SMALL_CAP),
        cost_estimate=pl.CostEstimate(flops=0, bytes_accessed=4 * PIECE * TILE, transcendentals=0),
        name="own_half",
    )(both, *after)


def keep_error(ids, grads, m1, m2, err, weights, part, before=None):
    width = 512
    tiles = width // TILE
    steps = HALF // width

    def kernel(ids_ref, g0, g1, g2, m1_ref, m2_ref, e_ref, w_ref, *rest):
        out, flag, kept, sems = rest[-4:]
        flag[...] = jnp.zeros_like(flag)
        copies = []
        for i in range(steps):
            for j in range(tiles):
                at = slice(width * i + TILE * j, width * i + TILE * (j + 1))
                to = slice(part * HALF + at.start, part * HALF + at.stop)
                g = total([r.at[:, at] for r in (g0, g1, g2)])
                kept[:, at] = accrue(g, m1_ref[:, to], m2_ref[:, to], e_ref[:, to], w_ref[:, to])
            for k in range(SLOTS):
                j = ids_ref[k] - part * (HALF // TILE) - i * tiles

                @pl.when((j >= 0) & (j < tiles))
                def _():
                    kept[:, pl.ds(pl.multiple_of(width * i + j * TILE, TILE), TILE)] = jnp.zeros((COLS, TILE), BF)

            copies.append(
                pltpu.make_async_copy(
                    kept.at[:, pl.ds(width * i, width)],
                    out.at[:, pl.ds(part * HALF + width * i, width)],
                    sems.at[i],
                )
            )
            copies[-1].start()
        for c in copies:
            c.wait()

    hbm = pl.BlockSpec(memory_space=pltpu.HBM)
    more = [] if before is None else [before]
    return pl.pallas_call(
        kernel,
        out_shape=[jax.ShapeDtypeStruct((COLS, FEATS), BF), jax.ShapeDtypeStruct((8, TILE), F32)],
        in_specs=[pl.BlockSpec(memory_space=pltpu.SMEM)] + [VMEM] * 7 + [hbm] * len(more),
        out_specs=[hbm, VMEM],
        input_output_aliases={8: 0} if more else {},
        scratch_shapes=[pltpu.VMEM((COLS, HALF), BF), pltpu.SemaphoreType.DMA((steps,))],
        compiler_params=pltpu.CompilerParams(vmem_limit_bytes=SMALL_CAP),
        cost_estimate=pl.CostEstimate(flops=20 * COLS * HALF, bytes_accessed=5 << 20, transcendentals=0),
        name="keep_error",
    )(ids, *grads, m1, m2, err, weights, *more)


def add_tiles(pieces, after):
    n = len(pieces)
    halves = sum(p.shape[0] // PIECE for p in pieces)

    def kernel(*refs):
        ins, (out, acc, listed) = refs[:n], refs[-3:]
        where = [(ref, h * PIECE) for ref in ins for h in range(ref.shape[0] // PIECE)]
        for at, (ref, row) in enumerate(where):
            for k, t in enumerate(get_ids(ref[row + SLOTS * COLS : row + PIECE])):
                listed[SLOTS * at + k] = t
        acc[...] = jnp.zeros_like(acc)
        for at, (ref, row) in enumerate(where):
            for k in range(SLOTS):
                t = listed[SLOTS * at + k]

                @pl.when(t >= 0)
                def _():
                    lanes = pl.ds(pl.multiple_of(t * TILE, TILE), TILE)
                    begin = row + COLS * k
                    acc[:, lanes] = acc[:, lanes] + ref[begin : begin + COLS].astype(F32)

        out[...] = (acc[...] * (1.0 / 16.0)).astype(BF)

    return pl.pallas_call(
        kernel,
        out_shape=jax.ShapeDtypeStruct((COLS, FEATS), BF),
        in_specs=[VMEM] * n + [pl.BlockSpec(memory_space=pl.ANY)] * len(after),
        scratch_shapes=[pltpu.VMEM((COLS, FEATS), F32), pltpu.SMEM((halves * SLOTS,), jnp.int32)],
        compiler_params=pltpu.CompilerParams(vmem_limit_bytes=SMALL_CAP),
        cost_estimate=pl.CostEstimate(flops=64 * 64 * 128, bytes_accessed=3 << 20, transcendentals=0),
        name="add_tiles",
    )(*pieces, *after)


def outer(mine, other, weights, momentum):
    width = 512
    steps = FEATS // width

    def kernel(m_ref, o_ref, w_ref, v_ref, w_out, v_out, w_new, v_new, sems):
        copies = []
        for i in range(steps):
            at = slice(width * i, width * (i + 1))
            agg = m_ref[:, at].astype(F32) + o_ref[:, at].astype(F32)
            vel = 0.9 * v_ref[:, at].astype(F32) + agg
            w_new[:, at] = w_ref[:, at] - 0.7 * (agg + 0.9 * vel)
            v_new[:, at] = vel.astype(BF)
            lanes = pl.ds(width * i, width)
            copies.append(pltpu.make_async_copy(w_new.at[:, lanes], w_out.at[:, lanes], sems.at[0, i]))
            copies.append(pltpu.make_async_copy(v_new.at[:, lanes], v_out.at[:, lanes], sems.at[1, i]))
            copies[-2].start()
            copies[-1].start()
        for c in copies:
            c.wait()

    hbm = pl.BlockSpec(memory_space=pltpu.HBM)
    return pl.pallas_call(
        kernel,
        out_shape=[jax.ShapeDtypeStruct((COLS, FEATS), F32), jax.ShapeDtypeStruct((COLS, FEATS), BF)],
        in_specs=[VMEM] * 4,
        out_specs=[hbm, hbm],
        scratch_shapes=[pltpu.VMEM((COLS, FEATS), F32), pltpu.VMEM((COLS, FEATS), BF), pltpu.SemaphoreType.DMA((2, steps))],
        compiler_params=pltpu.CompilerParams(vmem_limit_bytes=SMALL_CAP),
        cost_estimate=pl.CostEstimate(flops=6 * COLS * FEATS, bytes_accessed=8 << 20, transcendentals=0),
        name="outer",
    )(mine, other, weights, momentum)


def per_device(tokens, out_grad, weights, moment_one, moment_two, error_buf, momentum, tile_lists):
    tp = lax.axis_index("tp")
    ids = tile_lists[0, 0]
    place = jnp.concatenate([jnp.stack([tp // N, lax.rem(tp, N)]).astype(jnp.int32), ids])
    pos = place[:2]
    tok = tokens[0]
    og4 = out_grad[0].reshape(N, N, ROWS, COLS)
    state = (moment_one[0], moment_two[0], error_buf[0], weights)

    m = pack(place, tok, og4)
    yp, ym, xp, xm = along_y(m[0], 1), along_y(m[1], 3), along_x(m[2], 1), along_x(m[3], 3)
    y1, y2 = along_y(relay(yp, 1), 1), along_y(relay(ym, 3), 3)
    x1, x2 = along_x(relay(xp, 1), 1), along_x(relay(xm, 3), 3)

    ra = gather(pos, ids, og4, xp, xm, tok, yp, ym, 0)
    rb = gather(pos, ids, og4, yp, ym, tok, xp, xm, 1)
    pa = partials(pos, ra, x1, x2, y1, y2, 0, rb[1])
    sa = [pa[3], along_x(pa[5], 1), along_x(pa[4], 3), along_x(pa[6], 2)]
    pb = partials(pos, rb, y1, y2, x1, x2, 1, pa[3])
    (op_b,) = tied([pb[6]], sa[1:2])
    sb = [pb[3], along_y(pb[5], 1), along_y(pb[4], 3), along_y(op_b, 2)]
    near_a, far_a = add_beyond(pa[1], pa[2], sa[1], sa[2])
    near_b, far_b = add_beyond(pb[1], pb[2], sb[1], sb[2])
    ga = [pa[0], along_x(far_a, 1), along_x(near_a, 3)]
    gb = [pb[0], along_y(far_b, 1), along_y(near_b, 3)]

    mine = sent_tiles(ids, sa + sb, *state)
    own = pair(mine, across(mine))
    z1, z2 = onward(own, 1), onward(own, 2)
    z3, z4 = onward(z2, 1), onward(own_half(z2), 2)
    error_new, flag = keep_error(ids, gb, *state, 1)
    error_new, flag = keep_error(ids, ga, *state, 0, error_new)
    agg = add_tiles([mine, z1, z2, z3, z4], [flag])
    weights_new, momentum_new = outer(agg, across(agg), weights, momentum)

    return (weights_new, error_new[None], momentum_new)


def solution(mesh):
    return jax.shard_map(
        per_device,
        mesh=mesh,
        in_specs=(
            P("rep", "tp", None),
            P("rep", None, "tp"),
            P("tp", None),
            P("rep", "tp", None),
            P("rep", "tp", None),
            P("rep", "tp", None),
            P("tp", None),
            P("rep", "tp", None),
        ),
        out_specs=(P("tp", None), P("rep", "tp", None), P("tp", None)),
        check_vma=False,
    )
```
